32 devices in a mesh: groups: 2 (over x), expert: 16 (over z, y, core).
Axes of the slice: x: 2, y: 2, z: 4, core: 2. Of those that a mesh axis runs over, the one named last changes fastest.
Arguments:
- tokens: bfloat16 [4096, 2048], P(('groups', 'expert')), parts along dimension 0, may hold values from -6 to 6
- cotangent: bfloat16 [4096, 2048], P(('groups', 'expert')), parts along dimension 0, may hold values from -6 to 6
- route_probs: bfloat16 [4096, 2], P(('groups', 'expert')), parts along dimension 0, may hold values from 0.099609375 to 1
- expert_ids: int32 [4096, 2], P(('groups', 'expert')), parts along dimension 0, may hold values from 0 to 7, all different within a row; in each aligned block of 128 rows (0 to 127, 128 to 255, ...) at most 64 rows name the same one
- w_gate: bfloat16 [32, 2048, 384], P(('groups', 'expert')), parts along dimension 0, may hold values from -0.125 to 0.125
- w_up: bfloat16 [32, 2048, 384], P(('groups', 'expert')), parts along dimension 0, may hold values from -0.125 to 0.125
- w_down: bfloat16 [32, 384, 2048], P(('groups', 'expert')), parts along dimension 0, may hold values from -0.21875 to 0.21875
Outputs:
- token_grad: bfloat16 [4096, 2048], P(('groups', 'expert')), parts along dimension 0
- prob_grad: bfloat16 [4096, 2], P(('groups', 'expert')), parts along dimension 0
- gate_wgrad: bfloat16 [32, 2048, 384], P(('groups', 'expert')), parts along dimension 0
- up_wgrad: bfloat16 [32, 2048, 384], P(('groups', 'expert')), parts along dimension 0
- down_wgrad: bfloat16 [32, 384, 2048], P(('groups', 'expert')), parts along dimension 0
The draws below stay inside these ranges and needn't reach their ends.
There are 2 independent parts, one for each index of `groups`. The reference program is written for one: setup_inputs(seed, part) draws one part's arguments, and reference() takes and returns one part's arrays. A program takes and returns all parts, laid end to end along the dimension named above; each array names one. Nothing has to cross between parts.
Inputs may be any that keep to these rules, and one draw needn't show every extreme that they name: `expert_ids`: A token's 2 experts are distinct. Among the 128 tokens of one device (aligned blocks of rows), no expert is named by more than 64 tokens, a bound that some block reaches.
All inputs are finite; a program needn't handle non-finite values.
Results may differ from the reference program's by a relative error of at most 0.0095.
Values may be sent and summed in bfloat16 or wider, within the bound.
A program may use at most 128 MiB of HBM per device.

```python
import math
import jax
import jax.numpy as jnp
import numpy as np
from jax import lax

D = 2048
FF = 768
TOP = 2
TOK_DEV = 128
EXPERTS = 8
CAP = 64
TOKENS = 2048


def levels(own_key, extent, split, smallest, top_value):
    def one(position, parts):
        steps = jax.random.uniform(jax.random.fold_in(jax.random.fold_in(own_key, 6), position), (parts,), jnp.float32, smallest / len(split), top_value / len(split))
        return jnp.repeat(jnp.exp(steps), extent[position] // parts).reshape((-1,) + (1,) * (len(extent) - position - 1))

    gain = one(*split[0])
    for cut in split[1:]:
        gain = gain * one(*cut)
    return gain


def routed_block(rng, own, number, rows, number_of, top, most, slope):
    order = jax.random.permutation(rng, number_of)
    packed, usual = shares(number_of, rows * top, most, slope, True), shares(number_of, rows * top, most, slope, False)
    places = jnp.arange(number_of)

    def named(sizes, rotation):
        used = int((sizes > 0).sum())
        fixed = max(1, used // 4)
        shifted = fixed + (places - fixed + rotation * (used - fixed)) % max(1, number_of - fixed)
        return jnp.zeros((number_of,), jnp.int32).at[order[jnp.where(places < fixed, places, shifted)]].set(jnp.asarray(sizes, jnp.int32))

    sizes = jnp.where(number % 4 == 0, named(packed, number // 4), named(usual, number - number // 4 - 1))
    mixed = jax.random.permutation(jax.random.fold_in(own, 3), number_of)
    giver, receiver = mixed[0:number_of // 2 * 2:2], mixed[1:number_of // 2 * 2:2]
    room = jnp.minimum(sizes[giver] - 1, most - sizes[receiver]) // 2
    room = jnp.where((giver == order[0]) | (receiver == order[0]) | (sizes[receiver] == 0), 0, jnp.maximum(room, 0))
    shifted = jax.random.randint(jax.random.fold_in(own, 4), (number_of // 2,), 0, 1 << 20) % (room + 1)
    sizes = sizes.at[giver].add(-shifted).at[receiver].add(shifted)
    labels = jnp.searchsorted(jnp.cumsum(sizes), jnp.arange(rows * top), side="right").astype(jnp.int32)
    listing = labels.reshape(top, rows).T
    listing = listing[jax.random.permutation(jax.random.fold_in(own, 1), rows)]
    rotation = jax.random.randint(jax.random.fold_in(own, 2), (rows, 1), 0, top)
    return jnp.take_along_axis(listing, (jnp.arange(top)[None, :] + rotation) % top, axis=1)


def shares(amount, total, reach, lean, full):
    weights = [(1 << 20) // math.isqrt(grade ** lean) + 1 for grade in range(1, amount + 1)]
    largest = reach if full else min(reach, max(-(-total // amount), total * weights[0] // sum(weights)))
    least = 1 if total - largest >= amount - 1 else 0
    given, surplus = [largest] + [least] * (amount - 1), total - largest - least * (amount - 1)
    while surplus > 0:
        candidates = [i for i in range(1, amount) if given[i] < largest] or [i for i in range(1, amount) if given[i] < reach]
        pool, left = sum([weights[i] for i in candidates]), surplus
        for i in candidates:
            addition = min(reach - given[i], max(1, left * weights[i] // pool), surplus)
            given[i] = given[i] + addition
            surplus = surplus - addition
    return np.array(given)


def normal_values(stream_key, shape, scale, limit, split=(), kind=jnp.bfloat16):
    entries = scale * jax.random.normal(stream_key, shape, jnp.float32)
    if split:
        entries = entries * levels(stream_key, shape, split, -0.22, 0.18)
    return jnp.clip(entries, -limit, limit).astype(kind)


def setup_inputs(seed: int = 0, part: int = 0) -> dict:
    key_list = jax.random.split(jax.random.key(seed), 8)
    part_splits = jax.random.split(jax.random.fold_in(key_list[7], part), 8)
    tokens = normal_values(part_splits[0], (TOKENS, D), 1.0, 6.0, ((0, 16),))
    cotangent = normal_values(part_splits[1], (TOKENS, D), 1.0, 6.0, ((0, 16),))
    route_probs = jnp.clip(0.099609375 + 0.9003906 * jax.random.uniform(part_splits[2], (TOKENS, TOP), jnp.float32) ** levels(part_splits[2], (TOKENS, TOP), ((0, 16),), -0.2, 0.2), 0.099609375, 1.0).astype(jnp.bfloat16)
    expert_ids_keys = jax.random.split(jax.random.fold_in(part_splits[3], 1), TOKENS // TOK_DEV)
    expert_ids_turns = jax.random.permutation(jax.random.fold_in(part_splits[3], 3), TOKENS // TOK_DEV)
    expert_ids = jax.vmap(lambda own, number: routed_block(jax.random.fold_in(part_splits[3], 2), own, number, TOK_DEV, EXPERTS, TOP, CAP, 1))(expert_ids_keys, expert_ids_turns).reshape((TOKENS, TOP))
    w_gate = normal_values(part_splits[4], (2 * EXPERTS, D, FF // 2), D ** -0.5, 0.125, ((0, 16),))
    w_up = normal_values(part_splits[5], (2 * EXPERTS, D, FF // 2), D ** -0.5, 0.125, ((0, 16),))
    w_down = normal_values(part_splits[6], (2 * EXPERTS, FF // 2, D), FF ** -0.5, 0.21875, ((0, 16),))
    return {"tokens": tokens, "cotangent": cotangent, "route_probs": route_probs, "expert_ids": expert_ids, "w_gate": w_gate, "w_up": w_up, "w_down": w_down}


def half_backward(rows_x, rows_g, rows_p, gate_half, up_half, down_half):
    pre_gate = jnp.dot(rows_x, gate_half, preferred_element_type=jnp.float32)
    pre_up = jnp.dot(rows_x, up_half, preferred_element_type=jnp.float32)
    sigma = jax.nn.sigmoid(pre_gate)
    active = pre_gate * sigma
    hidden = (active * pre_up).astype(jnp.bfloat16)
    back_hidden = jnp.dot(rows_g, down_half.T, preferred_element_type=jnp.float32)
    gate_part = jnp.sum(back_hidden * hidden.astype(jnp.float32), axis=1).astype(jnp.bfloat16)
    weight_rows = rows_p.astype(jnp.float32)[:, None]
    scaled_hidden = weight_rows * back_hidden
    grad_pre = (scaled_hidden * pre_up * sigma * (1.0 + pre_gate * (1.0 - sigma))).astype(jnp.bfloat16)
    grad_up = (scaled_hidden * active).astype(jnp.bfloat16)
    scaled_cot = (weight_rows * rows_g.astype(jnp.float32)).astype(jnp.bfloat16)
    down_grad = jnp.dot(hidden.T, scaled_cot, preferred_element_type=jnp.float32).astype(jnp.bfloat16)
    gate_grad = jnp.dot(rows_x.T, grad_pre, preferred_element_type=jnp.float32).astype(jnp.bfloat16)
    up_grad = jnp.dot(rows_x.T, grad_up, preferred_element_type=jnp.float32).astype(jnp.bfloat16)
    input_part = (jnp.dot(grad_pre, gate_half.T, preferred_element_type=jnp.float32)
                  + jnp.dot(grad_up, up_half.T, preferred_element_type=jnp.float32)).astype(jnp.bfloat16)
    return input_part, gate_part, gate_grad, up_grad, down_grad


def reference(tokens, cotangent, route_probs, expert_ids, w_gate, w_up, w_down):
    pair_count = TOKENS * TOP
    slot_count = 2 * EXPERTS * CAP
    flat_ids = expert_ids.reshape(-1).astype(jnp.int32)
    onehot = (flat_ids[:, None] == jnp.arange(EXPERTS, dtype=jnp.int32)[None, :]).astype(jnp.int32)
    ranks = jnp.sum((jnp.cumsum(onehot, axis=0) - 1) * onehot, axis=1).astype(jnp.int32)
    place = (flat_ids * slot_count + ranks).astype(jnp.int32)
    source = jnp.full((EXPERTS * slot_count,), pair_count, jnp.int32).at[place].set(
        jnp.arange(pair_count, dtype=jnp.int32))
    table = source.reshape(EXPERTS, slot_count)
    tok_pad = jnp.concatenate([tokens, jnp.zeros((1, D), tokens.dtype)], axis=0)
    cot_pad = jnp.concatenate([cotangent, jnp.zeros((1, D), cotangent.dtype)], axis=0)
    prob_pad = jnp.concatenate([route_probs.reshape(-1), jnp.zeros((1,), route_probs.dtype)], axis=0)

    def per_expert(index):
        column = table[index]
        rows_x = tok_pad[column // TOP]
        rows_g = cot_pad[column // TOP]
        rows_p = prob_pad[column]
        first = half_backward(rows_x, rows_g, rows_p, w_gate[2 * index], w_up[2 * index], w_down[2 * index])
        second = half_backward(rows_x, rows_g, rows_p, w_gate[2 * index + 1], w_up[2 * index + 1],
                               w_down[2 * index + 1])
        summed = (first[0].astype(jnp.float32) + second[0].astype(jnp.float32)).astype(jnp.bfloat16)
        gate_sum = (first[1].astype(jnp.float32) + second[1].astype(jnp.float32)).astype(jnp.bfloat16)
        return (summed, gate_sum, jnp.stack([first[2], second[2]]), jnp.stack([first[3], second[3]]),
                jnp.stack([first[4], second[4]]))

    summed, gate_sum, gate_grad, up_grad, down_grad = lax.map(per_expert, jnp.arange(EXPERTS, dtype=jnp.int32))
    pair_rows = summed.reshape(EXPERTS * slot_count, D)[place]
    token_grad = pair_rows.reshape(TOKENS, TOP, D).astype(jnp.float32).sum(axis=1).astype(jnp.bfloat16)
    prob_grad = gate_sum.reshape(-1)[place].reshape(TOKENS, TOP)
    return (token_grad, prob_grad, gate_grad.reshape(2 * EXPERTS, D, FF // 2),
            up_grad.reshape(2 * EXPERTS, D, FF // 2), down_grad.reshape(2 * EXPERTS, FF // 2, D))
```

```python
import jax
import jax.numpy as jnp
from jax import lax
from jax.experimental import pallas as pl
from jax.experimental.pallas import tpu as pltpu
from jax.sharding import PartitionSpec as P


def half_backward(rows_x, rows_g, rows_p, gate_half, up_half, down_half):
    pre_gate = jnp.dot(rows_x, gate_half, preferred_element_type=jnp.float32)
    pre_up = jnp.dot(rows_x, up_half, preferred_element_type=jnp.float32)
    sigma = jax.nn.sigmoid(pre_gate)
    active = pre_gate * sigma
    hidden = (active * pre_up).astype(jnp.bfloat16)
    back_hidden = jnp.dot(rows_g, down_half.T, preferred_element_type=jnp.float32)
    gate_part = jnp.sum(back_hidden * hidden.astype(jnp.float32), axis=1).astype(jnp.bfloat16)
    weight_rows = rows_p.astype(jnp.float32)[:, None]
    scaled_hidden = weight_rows * back_hidden
    grad_pre = (scaled_hidden * pre_up * sigma * (1.0 + pre_gate * (1.0 - sigma))).astype(
        jnp.bfloat16
    )
    grad_up = (scaled_hidden * active).astype(jnp.bfloat16)
    scaled_cot = (weight_rows * rows_g.astype(jnp.float32)).astype(jnp.bfloat16)
    down_grad = jnp.dot(hidden.T, scaled_cot, preferred_element_type=jnp.float32).astype(
        jnp.bfloat16
    )
    gate_grad = jnp.dot(rows_x.T, grad_pre, preferred_element_type=jnp.float32).astype(jnp.bfloat16)
    up_grad = jnp.dot(rows_x.T, grad_up, preferred_element_type=jnp.float32).astype(jnp.bfloat16)
    input_part = (
        jnp.dot(grad_pre, gate_half.T, preferred_element_type=jnp.float32)
        + jnp.dot(grad_up, up_half.T, preferred_element_type=jnp.float32)
    ).astype(jnp.bfloat16)
    return (input_part, gate_part, gate_grad, up_grad, down_grad)


def local(tokens, cotangent, route_probs, expert_ids, w_gate, w_up, w_down):
    tok_count = tokens.shape[0]
    d_model = tokens.shape[1]
    per_token = expert_ids.shape[1]
    devices = lax.axis_size("expert")
    experts = devices // 2
    capacity = 2 * (tok_count * per_token // experts)
    pair_count = tok_count * per_token
    flat_ids = expert_ids.reshape(-1)
    onehot = (flat_ids[:, None] == jnp.arange(experts, dtype=jnp.int32)[None, :]).astype(jnp.int32)
    ranks = jnp.sum((jnp.cumsum(onehot, axis=0) - 1) * onehot, axis=1)
    place = flat_ids * capacity + ranks
    source = (
        jnp.full((experts * capacity,), pair_count, jnp.int32)
        .at[place]
        .set(jnp.arange(pair_count, dtype=jnp.int32))
    )
    tok_pad = jnp.concatenate([tokens, jnp.zeros((1, d_model), tokens.dtype)], axis=0)
    cot_pad = jnp.concatenate([cotangent, jnp.zeros((1, d_model), cotangent.dtype)], axis=0)
    prob_pad = jnp.concatenate(
        [route_probs.reshape(-1), jnp.zeros((1,), route_probs.dtype)], axis=0
    )
    send_x = tok_pad[source // per_token]
    send_g = cot_pad[source // per_token]
    send_p = prob_pad[source]
    got_x, got_g, got_p = (
        lax.all_to_all(
            jnp.repeat(send_x.reshape(experts, capacity, d_model), 2, axis=0),
            "expert",
            split_axis=0,
            concat_axis=0,
            tiled=True,
        ),
        lax.all_to_all(
            jnp.repeat(send_g.reshape(experts, capacity, d_model), 2, axis=0),
            "expert",
            split_axis=0,
            concat_axis=0,
            tiled=True,
        ),
        lax.all_to_all(
            jnp.repeat(send_p.reshape(experts, capacity), 2, axis=0),
            "expert",
            split_axis=0,
            concat_axis=0,
            tiled=True,
        ),
    )
    input_part, gate_part, gate_grad, up_grad, down_grad = half_backward(
        got_x.reshape(-1, d_model),
        got_g.reshape(-1, d_model),
        got_p.reshape(-1),
        w_gate[0],
        w_up[0],
        w_down[0],
    )
    part_rows = input_part.reshape(devices, capacity, d_model)
    part_gate = gate_part.reshape(devices, capacity)
    back_rows, back_gate = (
        lax.all_to_all(part_rows, "expert", split_axis=0, concat_axis=0, tiled=True),
        lax.all_to_all(part_gate, "expert", split_axis=0, concat_axis=0, tiled=True),
    )
    result_rows = (
        back_rows.reshape(experts, 2, capacity, d_model)
        .astype(jnp.float32)
        .sum(axis=1)
        .astype(jnp.bfloat16)
        .reshape(-1, d_model)
    )
    result_gate = (
        back_gate.reshape(experts, 2, capacity)
        .astype(jnp.float32)
        .sum(axis=1)
        .astype(jnp.bfloat16)
        .reshape(-1)
    )
    pair_rows = result_rows[place]
    token_grad = (
        pair_rows.reshape(tok_count, per_token, d_model)
        .astype(jnp.float32)
        .sum(axis=1)
        .astype(jnp.bfloat16)
    )
    prob_grad = result_gate[place].reshape(tok_count, per_token)
    return (token_grad, prob_grad, gate_grad[None], up_grad[None], down_grad[None])


NZ, NY, NC = 4, 2, 2
NS = NZ * NY * NC
COLS = 512
LIMIT = 56 * 2**20


def place_of(index):
    return index // (NY * NC), (index // NC) % NY, index % NC


def index_of(z, y, c):
    return z * (NY * NC) + y * NC + c


def enter(me):
    barrier = pltpu.get_barrier_semaphore()

    def greet(i, carry):
        pl.semaphore_signal(
            barrier, inc=1, device_id={"expert": (me + i) % NS}, device_id_type=pl.DeviceIdType.MESH
        )
        return carry

    lax.fori_loop(1, NS, greet, 0)
    pl.semaphore_wait(barrier, NS - 1)


def remote(src, dst, send, recv, target):
    return pltpu.make_async_remote_copy(
        src_ref=src,
        dst_ref=dst,
        send_sem=send,
        recv_sem=recv,
        device_id={"expert": target},
        device_id_type=pl.DeviceIdType.MESH,
    )


def onehot_rows(metas, source, own, other, cap):
    slot = lax.broadcasted_iota(jnp.int32, (cap, metas.shape[2]), 0).astype(jnp.float32)
    mine = metas[source, pl.ds(own, 1), :]
    theirs = metas[source, pl.ds(other, 1), :]
    return jnp.concatenate([slot == mine, slot == theirs], axis=0).astype(jnp.bfloat16)


def dispatch_kernel(
    xg_ref, meta_ref, slots, metas, zbuf, ysend, loc_sem, meta_send, meta_recv,
    up_send, dn_send, z_recv, y_send, y_recv, c_send, c_recv,
):
    me = lax.axis_index("expert")
    z, y, c = place_of(me)
    own, other = z * NY + y, z * NY + (1 - y)
    cap = slots.shape[2]
    width = slots.shape[3]
    local_copy = pltpu.make_async_copy(xg_ref, zbuf.at[z], loc_sem)
    local_copy.start()
    metas[me] = meta_ref[...]
    enter(me)

    def meta_copy(source, target):
        return remote(metas.at[source], metas.at[source], meta_send.at[target], meta_recv.at[source], target)

    def give_meta(i, carry):
        meta_copy(me, (me + i) % NS).start()
        return carry

    def take_meta(i, carry):
        source = (me + i) % NS
        meta_copy(source, source).wait_recv()
        return carry

    def done_meta(i, carry):
        meta_copy(me, (me + i) % NS).wait_send()
        return carry

    local_copy.wait()

    def up_copy(zz, a):
        return remote(
            zbuf.at[zz, a], zbuf.at[zz, a], up_send.at[zz, a], z_recv.at[zz, a], index_of(z + 1, y, c)
        )

    def dn_copy(zz, a):
        return remote(
            zbuf.at[zz, a], zbuf.at[zz, a], dn_send.at[zz, a], z_recv.at[zz, a], index_of(z - 1, y, c)
        )

    def y_copy(zz, a):
        return remote(
            ysend.at[a, zz],
            slots.at[a, index_of(zz, y, c)],
            y_send.at[a, zz],
            y_recv.at[a, zz],
            index_of(z, 1 - y, c),
        )

    def c_copy(source, a):
        return remote(
            slots.at[a, source],
            slots.at[a, source],
            c_send.at[a, source],
            c_recv.at[a, source],
            index_of(z, y, 1 - c),
        )

    def forward(zz, a, d):
        if d > 0:
            pltpu.make_async_copy(zbuf.at[zz, a], zbuf.at[zz, a], z_recv.at[zz, a]).wait()

        @pl.when((zz <= z) & (z < NZ - 1))
        def _():
            up_copy(zz, a).start()

        @pl.when((zz >= z) & (z > 0))
        def _():
            dn_copy(zz, a).start()

    def pick(zz, a):
        source = index_of(zz, y, c)
        hot = onehot_rows(metas, source, own, other, cap)

        @pl.loop(0, width // COLS)
        def _(j):
            cols = pl.ds(pl.multiple_of(j * COLS, COLS), COLS)
            rows = jnp.dot(hot, zbuf[zz, a, :, cols], preferred_element_type=jnp.float32)
            rows = rows.astype(jnp.bfloat16)
            slots[a, source, :, cols] = rows[:cap]
            ysend[a, zz, :, cols] = rows[cap:]

        y_copy(zz, a).start()
        c_copy(source, a).start()

    def relay(zz, a):
        source = index_of(zz, 1 - y, c)
        pltpu.make_async_copy(slots.at[a, source], slots.at[a, source], y_recv.at[a, zz]).wait()
        c_copy(source, a).start()

    def each(d, fn):
        if d == 0:
            fn(z)
        else:
            pl.when(z >= d)(lambda: fn(z - d))
            pl.when(z + d < NZ)(lambda: fn(z + d))

    for a in range(2):
        forward(z, a, 0)
    lax.fori_loop(1, NS, give_meta, 0)
    lax.fori_loop(1, NS, take_meta, 0)
    for d in range(NZ):
        for a in range(2):

            def step(zz, a=a, d=d):
                if d > 0:
                    forward(zz, a, d)
                pick(zz, a)

            each(d, step)
            if d > 0:
                each(d - 1, lambda zz, a=a: relay(zz, a))
    for a in range(2):
        each(NZ - 1, lambda zz, a=a: relay(zz, a))

    def finish(zz, carry):
        for a in range(2):

            @pl.when((zz <= z) & (z < NZ - 1))
            def _():
                up_copy(zz, a).wait_send()

            @pl.when((zz >= z) & (z > 0))
            def _():
                dn_copy(zz, a).wait_send()

            y_copy(zz, a).wait_send()
            for yy in range(NY):
                c_copy(index_of(zz, yy, c), a).wait_send()
                c_copy(index_of(zz, yy, 1 - c), a).wait_recv()
        return carry

    lax.fori_loop(0, NZ, finish, 0)
    lax.fori_loop(1, NS, done_meta, 0)


def return_kernel(
    part_ref, gate_ref, metas, token_ref, gates, half, pairs, dense, came,
    h_send, h_recv, q_send, q_recv, y_send, y_recv, r_send, r_recv,
):
    me = lax.axis_index("expert")
    z, y, c = place_of(me)
    own, other = z * NY + y, z * NY + (1 - y)
    cap = part_ref.shape[1]
    width = part_ref.shape[2]
    gates[me] = gate_ref[me]
    enter(me)

    def h_copy(zz, yy):
        return remote(
            part_ref.at[index_of(zz, yy, 1 - c)],
            half.at[zz, yy],
            h_send.at[zz, yy],
            h_recv.at[zz, yy],
            index_of(z, y, 1 - c),
        )

    def q_copy(target):
        return remote(gate_ref.at[target], gates.at[me], q_send.at[target], q_recv.at[me], target)

    def y_copy(zz):
        return remote(
            pairs.at[zz, 2],
            pairs.at[zz, 1],
            y_send.at[zz],
            y_recv.at[zz],
            index_of(z, 1 - y, c),
        )

    def r_copy(zz, way):
        return remote(
            dense.at[zz],
            came.at[zz, way],
            r_send.at[zz],
            r_recv.at[zz, way],
            index_of(z - 1 if way == 0 else z + 1, y, c),
        )

    def each(d, fn):
        if d == 0:
            fn(z)
        else:
            pl.when(z >= d)(lambda: fn(z - d))
            pl.when(z + d < NZ)(lambda: fn(z + d))

    def start_halves(zz):
        for yy in range(NY):
            h_copy(zz, yy).start()

    for d in range(NZ - 1, -1, -1):
        each(d, start_halves)

    def give_gate(i, carry):
        q_copy((me + i) % NS).start()
        return carry

    lax.fori_loop(1, NS, give_gate, 0)

    def add_half(zz, yy, to):
        source = index_of(zz, yy, c)
        h_copy(zz, yy).wait_recv()

        @pl.loop(0, width // COLS)
        def _(j):
            cols = pl.ds(pl.multiple_of(j * COLS, COLS), COLS)
            pairs[zz, to, :, cols] = (
                part_ref[source, :, cols].astype(jnp.float32) + half[zz, yy, :, cols].astype(jnp.float32)
            ).astype(jnp.bfloat16)

    def sum_halves(zz):
        add_half(zz, 1 - y, 2)
        y_copy(zz).start()
        add_half(zz, y, 0)

    def arrival(zz, way):
        pltpu.make_async_copy(came.at[zz, way], came.at[zz, way], r_recv.at[zz, way]).wait()

    def spread(zz, ways, out):
        hot = onehot_rows(metas, index_of(zz, y, c), own, other, cap)
        tokens = hot.shape[1]

        @pl.loop(0, width // COLS)
        def _(j):
            cols = pl.ds(pl.multiple_of(j * COLS, COLS), COLS)
            rows = jnp.concatenate([pairs[zz, 0, :, cols], pairs[zz, 1, :, cols]], axis=0)
            total = lax.dot_general(
                hot, rows, (((0,), (0,)), ((), ())), preferred_element_type=jnp.float32
            )
            out[:, cols] = total.astype(jnp.bfloat16)

        def add(way):
            arrival(zz, way)

            @pl.loop(0, width // COLS)
            def _(j):
                cols = pl.ds(pl.multiple_of(j * COLS, COLS), COLS)
                out[:, cols] = (
                    out[:, cols].astype(jnp.float32) + came[zz, way, :, cols].astype(jnp.float32)
                ).astype(jnp.bfloat16)

        for way in ways:
            if way == 0:
                pl.when(z < NZ - 1)(lambda: add(0))
            else:
                pl.when(z > 0)(lambda: add(1))

    for d in range(NZ - 1, -1, -1):
        each(d, sum_halves)
    for d in range(NZ - 1, 0, -1):

        @pl.when(z >= d)
        def _(d=d):
            zz = z - d
            y_copy(zz).wait_recv()
            spread(zz, (0,), dense.at[zz])
            r_copy(zz, 0).start()

        @pl.when(z + d < NZ)
        def _(d=d):
            zz = z + d
            y_copy(zz).wait_recv()
            spread(zz, (1,), dense.at[zz])
            r_copy(zz, 1).start()

    y_copy(z).wait_recv()
    spread(z, (0, 1), token_ref)

    def finish(zz, carry):
        for yy in range(NY):
            h_copy(zz, yy).wait_send()
        y_copy(zz).wait_send()

        @pl.when(zz < z)
        def _():
            r_copy(zz, 0).wait_send()

        @pl.when(zz > z)
        def _():
            r_copy(zz, 1).wait_send()

        return carry

    lax.fori_loop(0, NZ, finish, 0)

    def done_gate(i, carry):
        q_copy((me + i) % NS).wait_send()
        source = (me + i) % NS
        pltpu.make_async_copy(gates.at[source], gates.at[source], q_recv.at[source]).wait()
        return carry

    lax.fori_loop(1, NS, done_gate, 0)


def route_tables(route_probs, expert_ids, experts):
    tok_count = expert_ids.shape[0]
    names = jnp.arange(experts, dtype=jnp.int32)
    hit = expert_ids.T[:, None, :] == names[None, :, None]
    routed = jnp.any(hit, axis=0)
    order = jnp.arange(tok_count, dtype=jnp.int32)
    before = (order[:, None] < order[None, :]).astype(jnp.bfloat16)
    rank = jnp.dot(routed.astype(jnp.bfloat16), before, preferred_element_type=jnp.float32)
    slot = jnp.where(routed, rank, -1.0)
    prob = jnp.sum(jnp.where(hit, route_probs.T.astype(jnp.float32)[:, None, :], 0.0), axis=0)
    return hit, jnp.concatenate([slot, prob], axis=0)


def local_chips(tokens, cotangent, route_probs, expert_ids, w_gate, w_up, w_down):
    tok_count, d_model = tokens.shape
    per_token = expert_ids.shape[1]
    experts = NS // 2
    cap = 2 * (tok_count * per_token // experts)
    hit, meta = route_tables(route_probs, expert_ids, experts)
    vmem = pl.BlockSpec(memory_space=pltpu.VMEM)
    hbm = pl.BlockSpec(memory_space=pl.ANY)
    dma = pltpu.SemaphoreType.DMA
    slots, metas = pl.pallas_call(
        dispatch_kernel,
        out_shape=(
            jax.ShapeDtypeStruct((2, NS, cap, d_model), jnp.bfloat16),
            jax.ShapeDtypeStruct((NS,) + meta.shape, jnp.float32),
        ),
        in_specs=[hbm, vmem],
        out_specs=(vmem, vmem),
        scratch_shapes=[
            pltpu.VMEM((NZ, 2, tok_count, d_model), jnp.bfloat16),
            pltpu.VMEM((2, NZ, cap, d_model), jnp.bfloat16),
            dma(()),
            dma((NS,)),
            dma((NS,)),
            dma((NZ, 2)),
            dma((NZ, 2)),
            dma((NZ, 2)),
            dma((2, NZ)),
            dma((2, NZ)),
            dma((2, NS)),
            dma((2, NS)),
        ],
        compiler_params=pltpu.CompilerParams(
            collective_id=0, has_side_effects=True, vmem_limit_bytes=LIMIT
        ),
    )(jnp.stack([tokens, cotangent]), meta)
    expert = lax.axis_index("expert") // 2
    my_slot = lax.dynamic_index_in_dim(metas, expert, 1, keepdims=False)
    my_prob = lax.dynamic_index_in_dim(metas, expert + experts, 1, keepdims=False)
    number = jnp.arange(cap, dtype=jnp.int32).astype(jnp.float32)
    hot = my_slot[:, None, :] == number[None, :, None]
    rows_p = jnp.sum(jnp.where(hot, my_prob[:, None, :], 0.0), axis=2).reshape(-1)
    input_part, gate_part, gate_grad, up_grad, down_grad = half_backward(
        slots[0].reshape(-1, d_model),
        slots[1].reshape(-1, d_model),
        rows_p,
        w_gate[0],
        w_up[0],
        w_down[0],
    )
    gate_slot = gate_part.reshape(NS, cap).astype(jnp.float32)
    gate_tok = jnp.sum(jnp.where(hot, gate_slot[:, :, None], 0.0), axis=1)
    gate_tok = jnp.broadcast_to(gate_tok[:, None, :], (NS, 8, tok_count))
    token_grad, gates = pl.pallas_call(
        return_kernel,
        out_shape=(
            jax.ShapeDtypeStruct((tok_count, d_model), jnp.bfloat16),
            jax.ShapeDtypeStruct((NS, 8, tok_count), jnp.float32),
        ),
        in_specs=[vmem, vmem, vmem],
        out_specs=(vmem, vmem),
        scratch_shapes=[
            pltpu.VMEM((NZ, NY, cap, d_model), jnp.bfloat16),
            pltpu.VMEM((NZ, 3, cap, d_model), jnp.bfloat16),
            pltpu.VMEM((NZ, tok_count, d_model), jnp.bfloat16),
            pltpu.VMEM((NZ, 2, tok_count, d_model), jnp.bfloat16),
            dma((NZ, NY)),
            dma((NZ, NY)),
            dma((NS,)),
            dma((NS,)),
            dma((NZ,)),
            dma((NZ,)),
            dma((NZ,)),
            dma((NZ, 2)),
        ],
        compiler_params=pltpu.CompilerParams(
            collective_id=1, has_side_effects=True, vmem_limit_bytes=LIMIT
        ),
    )(input_part.reshape(NS, cap, d_model), gate_tok, metas)
    both = gates[:, 0, :].reshape(experts, 2, tok_count).sum(axis=1)
    prob_grad = jnp.sum(jnp.where(hit, both[None], 0.0), axis=1).T.astype(jnp.bfloat16)
    return (token_grad, prob_grad, gate_grad[None], up_grad[None], down_grad[None])


def solution(mesh):
    in_specs = (
        P(("groups", "expert"), None),
        P(("groups", "expert"), None),
        P(("groups", "expert"), None),
        P(("groups", "expert"), None),
        P(("groups", "expert"), None, None),
        P(("groups", "expert"), None, None),
        P(("groups", "expert"), None, None),
    )
    out_specs = (
        P(("groups", "expert"), None),
        P(("groups", "expert"), None),
        P(("groups", "expert"), None, None),
        P(("groups", "expert"), None, None),
        P(("groups", "expert"), None, None),
    )
    body = local_chips if mesh.shape["expert"] == NS else local
    return jax.shard_map(body, mesh=mesh, in_specs=in_specs, out_specs=out_specs, check_vma=False)
```

```python
import jax
import jax.numpy as jnp
from jax import lax
from jax.experimental import pallas as pl
from jax.experimental.pallas import tpu as pltpu
from jax.sharding import PartitionSpec as P


def half_backward(rows_x, rows_g, rows_p, gate_half, up_half, down_half):
    pre_gate = jnp.dot(rows_x, gate_half, preferred_element_type=jnp.float32)
    pre_up = jnp.dot(rows_x, up_half, preferred_element_type=jnp.float32)
    sigma = jax.nn.sigmoid(pre_gate)
    active = pre_gate * sigma
    hidden = (active * pre_up).astype(jnp.bfloat16)
    back_hidden = jnp.dot(rows_g, down_half.T, preferred_element_type=jnp.float32)
    gate_part = jnp.sum(back_hidden * hidden.astype(jnp.float32), axis=1).astype(jnp.bfloat16)
    weight_rows = rows_p.astype(jnp.float32)[:, None]
    scaled_hidden = weight_rows * back_hidden
    grad_pre = (scaled_hidden * pre_up * sigma * (1.0 + pre_gate * (1.0 - sigma))).astype(
        jnp.bfloat16
    )
    grad_up = (scaled_hidden * active).astype(jnp.bfloat16)
    scaled_cot = (weight_rows * rows_g.astype(jnp.float32)).astype(jnp.bfloat16)
    down_grad = jnp.dot(hidden.T, scaled_cot, preferred_element_type=jnp.float32).astype(
        jnp.bfloat16
    )
    gate_grad = jnp.dot(rows_x.T, grad_pre, preferred_element_type=jnp.float32).astype(jnp.bfloat16)
    up_grad = jnp.dot(rows_x.T, grad_up, preferred_element_type=jnp.float32).astype(jnp.bfloat16)
    input_part = (
        jnp.dot(grad_pre, gate_half.T, preferred_element_type=jnp.float32)
        + jnp.dot(grad_up, up_half.T, preferred_element_type=jnp.float32)
    ).astype(jnp.bfloat16)
    return (input_part, gate_part, gate_grad, up_grad, down_grad)


def local(tokens, cotangent, route_probs, expert_ids, w_gate, w_up, w_down):
    tok_count = tokens.shape[0]
    d_model = tokens.shape[1]
    per_token = expert_ids.shape[1]
    devices = lax.axis_size("expert")
    experts = devices // 2
    capacity = 2 * (tok_count * per_token // experts)
    pair_count = tok_count * per_token
    flat_ids = expert_ids.reshape(-1)
    onehot = (flat_ids[:, None] == jnp.arange(experts, dtype=jnp.int32)[None, :]).astype(jnp.int32)
    ranks = jnp.sum((jnp.cumsum(onehot, axis=0) - 1) * onehot, axis=1)
    place = flat_ids * capacity + ranks
    source = (
        jnp.full((experts * capacity,), pair_count, jnp.int32)
        .at[place]
        .set(jnp.arange(pair_count, dtype=jnp.int32))
    )
    tok_pad = jnp.concatenate([tokens, jnp.zeros((1, d_model), tokens.dtype)], axis=0)
    cot_pad = jnp.concatenate([cotangent, jnp.zeros((1, d_model), cotangent.dtype)], axis=0)
    prob_pad = jnp.concatenate(
        [route_probs.reshape(-1), jnp.zeros((1,), route_probs.dtype)], axis=0
    )
    send_x = tok_pad[source // per_token]
    send_g = cot_pad[source // per_token]
    send_p = prob_pad[source]
    got_x, got_g, got_p = (
        lax.all_to_all(
            jnp.repeat(send_x.reshape(experts, capacity, d_model), 2, axis=0),
            "expert",
            split_axis=0,
            concat_axis=0,
            tiled=True,
        ),
        lax.all_to_all(
            jnp.repeat(send_g.reshape(experts, capacity, d_model), 2, axis=0),
            "expert",
            split_axis=0,
            concat_axis=0,
            tiled=True,
        ),
        lax.all_to_all(
            jnp.repeat(send_p.reshape(experts, capacity), 2, axis=0),
            "expert",
            split_axis=0,
            concat_axis=0,
            tiled=True,
        ),
    )
    input_part, gate_part, gate_grad, up_grad, down_grad = half_backward(
        got_x.reshape(-1, d_model),
        got_g.reshape(-1, d_model),
        got_p.reshape(-1),
        w_gate[0],
        w_up[0],
        w_down[0],
    )
    part_rows = input_part.reshape(devices, capacity, d_model)
    part_gate = gate_part.reshape(devices, capacity)
    back_rows, back_gate = (
        lax.all_to_all(part_rows, "expert", split_axis=0, concat_axis=0, tiled=True),
        lax.all_to_all(part_gate, "expert", split_axis=0, concat_axis=0, tiled=True),
    )
    result_rows = (
        back_rows.reshape(experts, 2, capacity, d_model)
        .astype(jnp.float32)
        .sum(axis=1)
        .astype(jnp.bfloat16)
        .reshape(-1, d_model)
    )
    result_gate = (
        back_gate.reshape(experts, 2, capacity)
        .astype(jnp.float32)
        .sum(axis=1)
        .astype(jnp.bfloat16)
        .reshape(-1)
    )
    pair_rows = result_rows[place]
    token_grad = (
        pair_rows.reshape(tok_count, per_token, d_model)
        .astype(jnp.float32)
        .sum(axis=1)
        .astype(jnp.bfloat16)
    )
    prob_grad = result_gate[place].reshape(tok_count, per_token)
    return (token_grad, prob_grad, gate_grad[None], up_grad[None], down_grad[None])


NZ, NY, NC = 4, 2, 2
NS = NZ * NY * NC
COLS = 512
TILE = 256
LIMIT = 56 * 2**20


def place_of(index):
    return index // (NY * NC), (index // NC) % NY, index % NC


def index_of(z, y, c):
    return z * (NY * NC) + y * NC + c


def enter(me):
    barrier = pltpu.get_barrier_semaphore()

    def greet(i, carry):
        pl.semaphore_signal(
            barrier, inc=1, device_id={"expert": (me + i) % NS}, device_id_type=pl.DeviceIdType.MESH
        )
        return carry

    lax.fori_loop(1, NS, greet, 0)
    pl.semaphore_wait(barrier, NS - 1)


def remote(src, dst, send, recv, target):
    return pltpu.make_async_remote_copy(
        src_ref=src,
        dst_ref=dst,
        send_sem=send,
        recv_sem=recv,
        device_id={"expert": target},
        device_id_type=pl.DeviceIdType.MESH,
    )


def onehot_rows(metas, source, own, other, cap):
    slot = lax.broadcasted_iota(jnp.int32, (cap, metas.shape[2]), 0).astype(jnp.float32)
    mine = metas[source, pl.ds(own, 1), :]
    theirs = metas[source, pl.ds(other, 1), :]
    return jnp.concatenate([slot == mine, slot == theirs], axis=0).astype(jnp.bfloat16)


def fused_kernel(
    x_ref, g_ref, meta_ref, wg_ref, wu_ref, wd_ref,
    token_ref, gates, gate_out, up_out, down_out,
    metas, zbuf, ysend, slots, wgu, wd, gpu, hid_t, prob, part, gout, half, pairs, dense, came,
    loc_sem, meta_send, meta_recv, up_send, dn_send, z_recv, y_send, y_recv, c_send, c_recv,
    h_send, h_recv, q_send, q_recv, p_send, p_recv, r_send, r_recv,
):
    me = lax.axis_index("expert")
    z, y, c = place_of(me)
    own, other = z * NY + y, z * NY + (1 - y)
    experts = NS // 2
    cap, width = slots.shape[2], slots.shape[3]
    hidden = wd.shape[0]
    column = NY * NC
    rows_col = column * cap
    pieces = width // COLS
    loads = (
        pltpu.make_async_copy(x_ref, zbuf.at[z, 0], loc_sem.at[0]),
        pltpu.make_async_copy(g_ref, zbuf.at[z, 1], loc_sem.at[1]),
        pltpu.make_async_copy(wg_ref, wgu.at[:, pl.ds(0, hidden)], loc_sem.at[2]),
        pltpu.make_async_copy(wu_ref, wgu.at[:, pl.ds(hidden, hidden)], loc_sem.at[3]),
        pltpu.make_async_copy(wd_ref, wd, loc_sem.at[4]),
    )
    for load in loads:
        load.start()
    metas[me] = meta_ref[...]
    enter(me)

    def meta_copy(source, target):
        return remote(metas.at[source], metas.at[source], meta_send.at[target], meta_recv.at[source], target)

    def up_copy(zz, a):
        return remote(
            zbuf.at[zz, a], zbuf.at[zz, a], up_send.at[zz, a], z_recv.at[zz, a], index_of(z + 1, y, c)
        )

    def dn_copy(zz, a):
        return remote(
            zbuf.at[zz, a], zbuf.at[zz, a], dn_send.at[zz, a], z_recv.at[zz, a], index_of(z - 1, y, c)
        )

    def y_copy(zz, a):
        return remote(
            ysend.at[a, zz],
            slots.at[a, index_of(zz, y, c)],
            y_send.at[a, zz],
            y_recv.at[a, zz],
            index_of(z, 1 - y, c),
        )

    def c_copy(source, a):
        return remote(
            slots.at[a, source],
            slots.at[a, source],
            c_send.at[a, source],
            c_recv.at[a, source],
            index_of(z, y, 1 - c),
        )

    def h_copy(zz, yy):
        return remote(
            part.at[index_of(zz, yy, 1 - c)],
            half.at[zz, yy],
            h_send.at[zz, yy],
            h_recv.at[zz, yy],
            index_of(z, y, 1 - c),
        )

    def q_copy(target):
        return remote(gout.at[target], gates.at[me], q_send.at[target], q_recv.at[me], target)

    def p_copy(zz):
        return remote(
            pairs.at[zz, 2], pairs.at[zz, 1], p_send.at[zz], p_recv.at[zz], index_of(z, 1 - y, c)
        )

    def r_copy(zz, way, j):
        return remote(
            dense.at[zz, j],
            came.at[zz, way, j],
            r_send.at[zz, j],
            r_recv.at[zz, way, j],
            index_of(z - 1 + 2 * way, y, c),
        )

    def arrived(ref, sem):
        pltpu.make_async_copy(ref, ref, sem).wait()

    def both_ways(d, fn):
        @pl.loop(0, 2)
        def _(way):
            zz = z - d + 2 * d * way
            pl.when((zz >= 0) & (zz < NZ) & ((d > 0) | (way == 0)))(lambda: fn(zz))

    def forward(zz, a):
        @pl.when((zz <= z) & (z < NZ - 1))
        def _():
            up_copy(zz, a).start()

        @pl.when((zz >= z) & (z > 0))
        def _():
            dn_copy(zz, a).start()

    def pick(zz, a):
        source = index_of(zz, y, c)
        hot = onehot_rows(metas, source, own, other, cap)

        @pl.loop(0, pieces)
        def _(j):
            cols = pl.ds(pl.multiple_of(j * COLS, COLS), COLS)
            rows = jnp.dot(hot, zbuf[zz, a, :, cols], preferred_element_type=jnp.float32)
            rows = rows.astype(jnp.bfloat16)
            slots[a, source, :, cols] = rows[:cap]
            ysend[a, zz, :, cols] = rows[cap:]

        y_copy(zz, a).start()
        c_copy(source, a).start()

    def relay(zz, a):
        source = index_of(zz, 1 - y, c)
        arrived(slots.at[a, source], y_recv.at[a, zz])
        c_copy(source, a).start()

    def block(zz):
        base = zz * column
        hots = []
        probs = []
        for i in range(column):
            row = metas[base + i, pl.ds(own, 1), :]
            slot = lax.broadcasted_iota(jnp.int32, (cap, row.shape[1]), 0).astype(jnp.float32)
            hots.append(slot == row)
            weight = metas[base + i, pl.ds(own + experts, 1), :]
            probs.append(jnp.sum(jnp.where(hots[i], weight, 0.0), axis=1, keepdims=True))
        p = jnp.concatenate(probs, axis=0)
        prob[zz] = p
        rows_x = slots[0, pl.ds(base, column)].reshape(rows_col, width)
        pre = jnp.dot(rows_x, wgu[...], preferred_element_type=jnp.float32)
        pre_gate, pre_up = pre[:, :hidden], pre[:, hidden:]
        rows_g = slots[1, pl.ds(base, column)].reshape(rows_col, width)
        back = lax.dot_general(
            rows_g, wd[...], (((1,), (1,)), ((), ())), preferred_element_type=jnp.float32
        )
        sigma = jax.nn.sigmoid(pre_gate)
        active = pre_gate * sigma
        hid = (active * pre_up).astype(jnp.bfloat16)
        q = jnp.sum(back * hid.astype(jnp.float32), axis=1, keepdims=True)
        q = q.astype(jnp.bfloat16).astype(jnp.float32)
        scaled = p * back
        gpu[zz, :, :hidden] = (
            scaled * pre_up * sigma * (1.0 + pre_gate * (1.0 - sigma))
        ).astype(jnp.bfloat16)
        gpu[zz, :, hidden:] = (scaled * active).astype(jnp.bfloat16)
        hid_t[zz] = hid.T
        for i in range(column):
            gate = jnp.sum(jnp.where(hots[i], q[i * cap : (i + 1) * cap], 0.0), axis=0, keepdims=True)
            gout[base + i] = jnp.broadcast_to(gate, gout.shape[1:])

        @pl.loop(0, pieces)
        def _(j):
            cols = pl.ds(pl.multiple_of(j * COLS, COLS), COLS)
            grads = lax.dot_general(
                gpu[zz], wgu[cols, :], (((1,), (1,)), ((), ())), preferred_element_type=jnp.float32
            )
            part[pl.ds(base, column), :, cols] = grads.astype(jnp.bfloat16).reshape(column, cap, COLS)

    def add_half(zz, yy, to):
        source = index_of(zz, yy, c)
        h_copy(zz, yy).wait_recv()

        @pl.loop(0, pieces)
        def _(j):
            cols = pl.ds(pl.multiple_of(j * COLS, COLS), COLS)
            pairs[zz, to, :, cols] = (
                part[source, :, cols].astype(jnp.float32) + half[zz, yy, :, cols].astype(jnp.float32)
            ).astype(jnp.bfloat16)

    def gate_row(i, fn):
        pl.when(i != me)(lambda: fn(i))

    def spread(zz, j):
        cols = pl.ds(pl.multiple_of(j * COLS, COLS), COLS)
        hot = onehot_rows(metas, index_of(zz, y, c), own, other, cap)
        rows = jnp.concatenate([pairs[zz, 0, :, cols], pairs[zz, 1, :, cols]], axis=0)
        total = lax.dot_general(hot, rows, (((0,), (0,)), ((), ())), preferred_element_type=jnp.float32)
        return total.astype(jnp.bfloat16)

    def add_came(value, zz, way, j):
        arrived(came.at[zz, way, j], r_recv.at[zz, way, j])
        return (value.astype(jnp.float32) + came[zz, way, j].astype(jnp.float32)).astype(jnp.bfloat16)

    def chain(zz, relayed):
        way = jnp.where(zz < z, 0, 1)
        p_copy(zz).wait_recv()

        @pl.loop(0, pieces)
        def _(j):
            value = spread(zz, j)
            dense[zz, j] = add_came(value, zz, way, j) if relayed else value
            r_copy(zz, way, j).start()

    middle = (z > 0) & (z < NZ - 1)

    def process(zz):
        for a in range(2):
            relay(zz, a)
        for a in range(2):
            for yy in range(NY):
                c_copy(index_of(zz, yy, 1 - c), a).wait_recv()
        block(zz)
        for i in range(NY):
            h_copy(zz, (1 - y + i) % NY).start()
        for i in range(column):
            gate_row(zz * column + i, lambda target: q_copy(target).start())
        add_half(zz, 1 - y, 2)
        p_copy(zz).start()
        add_half(zz, y, 0)
        pl.when(jnp.logical_not(middle) & (zz != z))(lambda: chain(zz, False))

    loads[0].wait()
    forward(z, 0)
    loads[1].wait()
    forward(z, 1)

    def give_meta(i, carry):
        meta_copy(me, (me + i) % NS).start()
        return carry

    def take_meta(i, carry):
        source = (me + i) % NS
        meta_copy(source, source).wait_recv()
        return carry

    lax.fori_loop(1, NS, give_meta, 0)
    lax.fori_loop(1, NS, take_meta, 0)

    @pl.loop(0, NZ)
    def _(d):
        for a in range(2):

            def step(zz, a=a):
                @pl.when(d > 0)
                def _():
                    arrived(zbuf.at[zz, a], z_recv.at[zz, a])
                    forward(zz, a)

                pick(zz, a)

            both_ways(d, step)

        @pl.when(d == 0)
        def _():
            for load in loads[2:]:
                load.wait()

        both_ways(d, process)

    @pl.loop(0, width // TILE)
    def _(j):
        cols = pl.ds(pl.multiple_of(j * TILE, TILE), TILE)
        wide = jnp.zeros((TILE, 2 * hidden), jnp.float32)
        down = jnp.zeros((hidden, TILE), jnp.float32)
        for k in range(NZ):
            rows_x = slots[0, k * column : (k + 1) * column, :, cols].reshape(rows_col, TILE)
            wide += lax.dot_general(
                rows_x, gpu[k], (((0,), (0,)), ((), ())), preferred_element_type=jnp.float32
            )
            rows_g = slots[1, k * column : (k + 1) * column, :, cols].reshape(rows_col, TILE)
            scaled = (prob[k] * rows_g.astype(jnp.float32)).astype(jnp.bfloat16)
            down += jnp.dot(hid_t[k], scaled, preferred_element_type=jnp.float32)
        gate_out[cols, :] = wide[:, :hidden].astype(jnp.bfloat16)
        up_out[cols, :] = wide[:, hidden:].astype(jnp.bfloat16)
        down_out[:, cols] = down.astype(jnp.bfloat16)

    @pl.when(middle)
    def _():
        long_side = 1 - 2 * (z // 2)
        for i in range(NZ - 2):
            chain(z + long_side * (i + 1), True)
        chain(z - long_side, True)

    p_copy(z).wait_recv()

    @pl.loop(0, pieces)
    def _(j):
        cols = pl.ds(pl.multiple_of(j * COLS, COLS), COLS)
        token_ref[:, cols] = spread(z, j)

        @pl.when(z < NZ - 1)
        def _():
            token_ref[:, cols] = add_came(token_ref[:, cols], z, 0, j)

        @pl.when(z > 0)
        def _():
            token_ref[:, cols] = add_came(token_ref[:, cols], z, 1, j)

    gates[me] = gout[me]

    def finish(zz, carry):
        for a in range(2):

            @pl.when((zz <= z) & (z < NZ - 1))
            def _():
                up_copy(zz, a).wait_send()

            @pl.when((zz >= z) & (z > 0))
            def _():
                dn_copy(zz, a).wait_send()

            y_copy(zz, a).wait_send()
            for yy in range(NY):
                c_copy(index_of(zz, yy, c), a).wait_send()
        for yy in range(NY):
            h_copy(zz, yy).wait_send()
        p_copy(zz).wait_send()

        @pl.when(zz != z)
        def _():
            for j in range(pieces):
                r_copy(zz, jnp.where(zz < z, 0, 1), j).wait_send()

        return carry

    lax.fori_loop(0, NZ, finish, 0)

    def done(i, carry):
        target = (me + i) % NS
        meta_copy(me, target).wait_send()
        q_copy(target).wait_send()
        arrived(gates.at[target], q_recv.at[target])
        return carry

    lax.fori_loop(1, NS, done, 0)


def route_tables(route_probs, expert_ids, experts):
    tok_count = expert_ids.shape[0]
    names = jnp.arange(experts, dtype=jnp.int32)
    hit = expert_ids.T[:, None, :] == names[None, :, None]
    routed = jnp.any(hit, axis=0)
    order = jnp.arange(tok_count, dtype=jnp.int32)
    before = (order[:, None] < order[None, :]).astype(jnp.bfloat16)
    rank = jnp.dot(routed.astype(jnp.bfloat16), before, preferred_element_type=jnp.float32)
    slot = jnp.where(routed, rank, -1.0)
    prob = jnp.sum(jnp.where(hit, route_probs.T.astype(jnp.float32)[:, None, :], 0.0), axis=0)
    return hit, jnp.concatenate([slot, prob], axis=0)


def local_chips(tokens, cotangent, route_probs, expert_ids, w_gate, w_up, w_down):
    tok_count, d_model = tokens.shape
    per_token = expert_ids.shape[1]
    experts = NS // 2
    cap = 2 * (tok_count * per_token // experts)
    hit, meta = route_tables(route_probs, expert_ids, experts)
    hidden = w_down.shape[1]
    column = NY * NC
    pieces = d_model // COLS
    vmem = pl.BlockSpec(memory_space=pltpu.VMEM)
    hbm = pl.BlockSpec(memory_space=pl.ANY)
    dma = pltpu.SemaphoreType.DMA
    half_type = jnp.bfloat16
    token_grad, gates, gate_grad, up_grad, down_grad = pl.pallas_call(
        fused_kernel,
        out_shape=(
            jax.ShapeDtypeStruct((tok_count, d_model), half_type),
            jax.ShapeDtypeStruct((NS, 8, tok_count), jnp.float32),
            jax.ShapeDtypeStruct((d_model, hidden), half_type),
            jax.ShapeDtypeStruct((d_model, hidden), half_type),
            jax.ShapeDtypeStruct((hidden, d_model), half_type),
        ),
        in_specs=[hbm, hbm, vmem, hbm, hbm, hbm],
        out_specs=(vmem,) * 5,
        scratch_shapes=[
            pltpu.VMEM((NS,) + meta.shape, jnp.float32),
            pltpu.VMEM((NZ, 2, tok_count, d_model), half_type),
            pltpu.VMEM((2, NZ, cap, d_model), half_type),
            pltpu.VMEM((2, NS, cap, d_model), half_type),
            pltpu.VMEM((d_model, 2 * hidden), half_type),
            pltpu.VMEM((hidden, d_model), half_type),
            pltpu.VMEM((NZ, column * cap, 2 * hidden), half_type),
            pltpu.VMEM((NZ, hidden, column * cap), half_type),
            pltpu.VMEM((NZ, column * cap, 1), jnp.float32),
            pltpu.VMEM((NS, cap, d_model), half_type),
            pltpu.VMEM((NS, 8, tok_count), jnp.float32),
            pltpu.VMEM((NZ, NY, cap, d_model), half_type),
            pltpu.VMEM((NZ, 3, cap, d_model), half_type),
            pltpu.VMEM((NZ, pieces, tok_count, COLS), half_type),
            pltpu.VMEM((NZ, 2, pieces, tok_count, COLS), half_type),
            dma((5,)),
            dma((NS,)),
            dma((NS,)),
            dma((NZ, 2)),
            dma((NZ, 2)),
            dma((NZ, 2)),
            dma((2, NZ)),
            dma((2, NZ)),
            dma((2, NS)),
            dma((2, NS)),
            dma((NZ, NY)),
            dma((NZ, NY)),
            dma((NS,)),
            dma((NS,)),
            dma((NZ,)),
            dma((NZ,)),
            dma((NZ, pieces)),
            dma((NZ, 2, pieces)),
        ],
        compiler_params=pltpu.CompilerParams(
            collective_id=0, has_side_effects=True, vmem_limit_bytes=LIMIT
        ),
    )(tokens, cotangent, meta, w_gate[0], w_up[0], w_down[0])
    both = gates[:, 0, :].reshape(experts, 2, tok_count).sum(axis=1)
    prob_grad = jnp.sum(jnp.where(hit, both[None], 0.0), axis=1).T.astype(jnp.bfloat16)
    return (token_grad, prob_grad, gate_grad[None], up_grad[None], down_grad[None])


def solution(mesh):
    in_specs = (
        P(("groups", "expert"), None),
        P(("groups", "expert"), None),
        P(("groups", "expert"), None),
        P(("groups", "expert"), None),
        P(("groups", "expert"), None, None),
        P(("groups", "expert"), None, None),
        P(("groups", "expert"), None, None),
    )
    out_specs = (
        P(("groups", "expert"), None),
        P(("groups", "expert"), None),
        P(("groups", "expert"), None, None),
        P(("groups", "expert"), None, None),
        P(("groups", "expert"), None, None),
    )
    body = local_chips if mesh.shape["expert"] == NS else local
    return jax.shard_map(body, mesh=mesh, in_specs=in_specs, out_specs=out_specs, check_vma=False)
```

```python
import jax
import jax.numpy as jnp
from jax import lax
from jax.experimental import pallas as pl
from jax.experimental.pallas import tpu as pltpu
from jax.sharding import PartitionSpec as P


def half_backward(rows_x, rows_g, rows_p, gate_half, up_half, down_half):
    pre_gate = jnp.dot(rows_x, gate_half, preferred_element_type=jnp.float32)
    pre_up = jnp.dot(rows_x, up_half, preferred_element_type=jnp.float32)
    sigma = jax.nn.sigmoid(pre_gate)
    active = pre_gate * sigma
    hidden = (active * pre_up).astype(jnp.bfloat16)
    back_hidden = jnp.dot(rows_g, down_half.T, preferred_element_type=jnp.float32)
    gate_part = jnp.sum(back_hidden * hidden.astype(jnp.float32), axis=1).astype(jnp.bfloat16)
    weight_rows = rows_p.astype(jnp.float32)[:, None]
    scaled_hidden = weight_rows * back_hidden
    grad_pre = (scaled_hidden * pre_up * sigma * (1.0 + pre_gate * (1.0 - sigma))).astype(
        jnp.bfloat16
    )
    grad_up = (scaled_hidden * active).astype(jnp.bfloat16)
    scaled_cot = (weight_rows * rows_g.astype(jnp.float32)).astype(jnp.bfloat16)
    down_grad = jnp.dot(hidden.T, scaled_cot, preferred_element_type=jnp.float32).astype(
        jnp.bfloat16
    )
    gate_grad = jnp.dot(rows_x.T, grad_pre, preferred_element_type=jnp.float32).astype(jnp.bfloat16)
    up_grad = jnp.dot(rows_x.T, grad_up, preferred_element_type=jnp.float32).astype(jnp.bfloat16)
    input_part = (
        jnp.dot(grad_pre, gate_half.T, preferred_element_type=jnp.float32)
        + jnp.dot(grad_up, up_half.T, preferred_element_type=jnp.float32)
    ).astype(jnp.bfloat16)
    return (input_part, gate_part, gate_grad, up_grad, down_grad)


def local(tokens, cotangent, route_probs, expert_ids, w_gate, w_up, w_down):
    tok_count = tokens.shape[0]
    d_model = tokens.shape[1]
    per_token = expert_ids.shape[1]
    devices = lax.axis_size("expert")
    experts = devices // 2
    capacity = 2 * (tok_count * per_token // experts)
    pair_count = tok_count * per_token
    flat_ids = expert_ids.reshape(-1)
    onehot = (flat_ids[:, None] == jnp.arange(experts, dtype=jnp.int32)[None, :]).astype(jnp.int32)
    ranks = jnp.sum((jnp.cumsum(onehot, axis=0) - 1) * onehot, axis=1)
    place = flat_ids * capacity + ranks
    source = (
        jnp.full((experts * capacity,), pair_count, jnp.int32)
        .at[place]
        .set(jnp.arange(pair_count, dtype=jnp.int32))
    )
    tok_pad = jnp.concatenate([tokens, jnp.zeros((1, d_model), tokens.dtype)], axis=0)
    cot_pad = jnp.concatenate([cotangent, jnp.zeros((1, d_model), cotangent.dtype)], axis=0)
    prob_pad = jnp.concatenate(
        [route_probs.reshape(-1), jnp.zeros((1,), route_probs.dtype)], axis=0
    )
    send_x = tok_pad[source // per_token]
    send_g = cot_pad[source // per_token]
    send_p = prob_pad[source]
    got_x, got_g, got_p = (
        lax.all_to_all(
            jnp.repeat(send_x.reshape(experts, capacity, d_model), 2, axis=0),
            "expert",
            split_axis=0,
            concat_axis=0,
            tiled=True,
        ),
        lax.all_to_all(
            jnp.repeat(send_g.reshape(experts, capacity, d_model), 2, axis=0),
            "expert",
            split_axis=0,
            concat_axis=0,
            tiled=True,
        ),
        lax.all_to_all(
            jnp.repeat(send_p.reshape(experts, capacity), 2, axis=0),
            "expert",
            split_axis=0,
            concat_axis=0,
            tiled=True,
        ),
    )
    input_part, gate_part, gate_grad, up_grad, down_grad = half_backward(
        got_x.reshape(-1, d_model),
        got_g.reshape(-1, d_model),
        got_p.reshape(-1),
        w_gate[0],
        w_up[0],
        w_down[0],
    )
    part_rows = input_part.reshape(devices, capacity, d_model)
    part_gate = gate_part.reshape(devices, capacity)
    back_rows, back_gate = (
        lax.all_to_all(part_rows, "expert", split_axis=0, concat_axis=0, tiled=True),
        lax.all_to_all(part_gate, "expert", split_axis=0, concat_axis=0, tiled=True),
    )
    result_rows = (
        back_rows.reshape(experts, 2, capacity, d_model)
        .astype(jnp.float32)
        .sum(axis=1)
        .astype(jnp.bfloat16)
        .reshape(-1, d_model)
    )
    result_gate = (
        back_gate.reshape(experts, 2, capacity)
        .astype(jnp.float32)
        .sum(axis=1)
        .astype(jnp.bfloat16)
        .reshape(-1)
    )
    pair_rows = result_rows[place]
    token_grad = (
        pair_rows.reshape(tok_count, per_token, d_model)
        .astype(jnp.float32)
        .sum(axis=1)
        .astype(jnp.bfloat16)
    )
    prob_grad = result_gate[place].reshape(tok_count, per_token)
    return (token_grad, prob_grad, gate_grad[None], up_grad[None], down_grad[None])


NZ, NY, NC = 4, 2, 2
NS = NZ * NY * NC
COLS = 1024
TILE = 256
LIMIT = 56 * 2**20


def place_of(index):
    return index // (NY * NC), (index // NC) % NY, index % NC


def index_of(z, y, c):
    return z * (NY * NC) + y * NC + c


def enter(me):
    barrier = pltpu.get_barrier_semaphore()

    def greet(i, carry):
        pl.semaphore_signal(
            barrier, inc=1, device_id={"expert": (me + i) % NS}, device_id_type=pl.DeviceIdType.MESH
        )
        return carry

    lax.fori_loop(1, NS, greet, 0)
    pl.semaphore_wait(barrier, NS - 1)


def remote(src, dst, send, recv, target):
    return pltpu.make_async_remote_copy(
        src_ref=src,
        dst_ref=dst,
        send_sem=send,
        recv_sem=recv,
        device_id={"expert": target},
        device_id_type=pl.DeviceIdType.MESH,
    )


def onehot_rows(metas, source, own, other, cap):
    slot = lax.broadcasted_iota(jnp.int32, (cap, metas.shape[2]), 0).astype(jnp.float32)
    mine = metas[source, pl.ds(own, 1), :]
    theirs = metas[source, pl.ds(other, 1), :]
    return jnp.concatenate([slot == mine, slot == theirs], axis=0).astype(jnp.bfloat16)


def fused_kernel(
    x_ref, g_ref, meta_ref, wg_ref, wu_ref, wd_ref,
    token_ref, gates, gate_out, up_out, down_out,
    metas, zbuf, ysend, slots, wgu, wd, gpu, hid_t, prob, part, gout, half, pairs, dense, came,
    loc_sem, meta_send, meta_recv, up_send, dn_send, z_recv, y_send, y_recv, c_send, c_recv,
    h_send, h_recv, q_send, q_recv, p_send, p_recv, r_send, r_recv,
):
    me = lax.axis_index("expert")
    z, y, c = place_of(me)
    own, other = z * NY + y, z * NY + (1 - y)
    experts = NS // 2
    cap, width = slots.shape[2], slots.shape[3]
    hidden = wd.shape[0]
    column = NY * NC
    rows_col = column * cap
    pieces = width // COLS
    loads = (
        pltpu.make_async_copy(x_ref, zbuf.at[z, 0], loc_sem.at[0]),
        pltpu.make_async_copy(g_ref, zbuf.at[z, 1], loc_sem.at[1]),
        pltpu.make_async_copy(wg_ref, wgu.at[:, pl.ds(0, hidden)], loc_sem.at[2]),
        pltpu.make_async_copy(wu_ref, wgu.at[:, pl.ds(hidden, hidden)], loc_sem.at[3]),
        pltpu.make_async_copy(wd_ref, wd, loc_sem.at[4]),
    )
    for load in loads:
        load.start()
    metas[me] = meta_ref[...]
    enter(me)

    def meta_copy(source, target):
        return remote(metas.at[source], metas.at[source], meta_send.at[target], meta_recv.at[source], target)

    def up_copy(zz, a):
        return remote(
            zbuf.at[zz, a], zbuf.at[zz, a], up_send.at[zz, a], z_recv.at[zz, a], index_of(z + 1, y, c)
        )

    def dn_copy(zz, a):
        return remote(
            zbuf.at[zz, a], zbuf.at[zz, a], dn_send.at[zz, a], z_recv.at[zz, a], index_of(z - 1, y, c)
        )

    def y_copy(zz, a):
        return remote(
            ysend.at[a, zz],
            slots.at[a, index_of(zz, y, c)],
            y_send.at[a, zz],
            y_recv.at[a, zz],
            index_of(z, 1 - y, c),
        )

    def c_copy(source, a):
        return remote(
            slots.at[a, source],
            slots.at[a, source],
            c_send.at[a, source],
            c_recv.at[a, source],
            index_of(z, y, 1 - c),
        )

    def h_copy(zz, yy):
        return remote(
            part.at[index_of(zz, yy, 1 - c)],
            half.at[zz, yy],
            h_send.at[zz, yy],
            h_recv.at[zz, yy],
            index_of(z, y, 1 - c),
        )

    def q_copy(target):
        return remote(gout.at[target], gates.at[me], q_send.at[target], q_recv.at[me], target)

    def p_copy(zz):
        return remote(
            pairs.at[zz, 2], pairs.at[zz, 1], p_send.at[zz], p_recv.at[zz], index_of(z, 1 - y, c)
        )

    def r_copy(zz, way, j):
        return remote(
            dense.at[zz, j],
            came.at[zz, way, j],
            r_send.at[zz, j],
            r_recv.at[zz, way, j],
            index_of(z - 1 + 2 * way, y, c),
        )

    def arrived(ref, sem):
        pltpu.make_async_copy(ref, ref, sem).wait()

    def both_ways(d, fn):
        @pl.loop(0, 2)
        def _(way):
            zz = z - d + 2 * d * way
            pl.when((zz >= 0) & (zz < NZ) & ((d > 0) | (way == 0)))(lambda: fn(zz))

    def forward(zz, a):
        @pl.when((zz <= z) & (z < NZ - 1))
        def _():
            up_copy(zz, a).start()

        @pl.when((zz >= z) & (z > 0))
        def _():
            dn_copy(zz, a).start()

    def pick(zz, a):
        source = index_of(zz, y, c)
        hot = onehot_rows(metas, source, own, other, cap)

        @pl.loop(0, pieces)
        def _(j):
            cols = pl.ds(pl.multiple_of(j * COLS, COLS), COLS)
            rows = jnp.dot(hot, zbuf[zz, a, :, cols], preferred_element_type=jnp.float32)
            rows = rows.astype(jnp.bfloat16)
            slots[a, source, :, cols] = rows[:cap]
            ysend[a, zz, :, cols] = rows[cap:]

        y_copy(zz, a).start()
        c_copy(source, a).start()

    def relay(zz, a):
        source = index_of(zz, 1 - y, c)
        arrived(slots.at[a, source], y_recv.at[a, zz])
        c_copy(source, a).start()

    def block(zz):
        base = zz * column
        hots = []
        probs = []
        for i in range(column):
            row = metas[base + i, pl.ds(own, 1), :]
            slot = lax.broadcasted_iota(jnp.int32, (cap, row.shape[1]), 0).astype(jnp.float32)
            hots.append(slot == row)
            weight = metas[base + i, pl.ds(own + experts, 1), :]
            probs.append(jnp.sum(jnp.where(hots[i], weight, 0.0), axis=1, keepdims=True))
        p = jnp.concatenate(probs, axis=0)
        prob[zz] = p
        rows_x = slots[0, pl.ds(base, column)].reshape(rows_col, width)
        pre = jnp.dot(rows_x, wgu[...], preferred_element_type=jnp.float32)
        pre_gate, pre_up = pre[:, :hidden], pre[:, hidden:]
        rows_g = slots[1, pl.ds(base, column)].reshape(rows_col, width)
        back = lax.dot_general(
            rows_g, wd[...], (((1,), (1,)), ((), ())), preferred_element_type=jnp.float32
        )
        sigma = jax.nn.sigmoid(pre_gate)
        active = pre_gate * sigma
        hid = (active * pre_up).astype(jnp.bfloat16)
        q = jnp.sum(back * hid.astype(jnp.float32), axis=1, keepdims=True)
        q = q.astype(jnp.bfloat16).astype(jnp.float32)
        scaled = p * back
        gpu[zz, :, :hidden] = (
            scaled * pre_up * sigma * (1.0 + pre_gate * (1.0 - sigma))
        ).astype(jnp.bfloat16)
        gpu[zz, :, hidden:] = (scaled * active).astype(jnp.bfloat16)
        hid_t[zz] = hid.T
        for i in range(column):
            gate = jnp.sum(jnp.where(hots[i], q[i * cap : (i + 1) * cap], 0.0), axis=0, keepdims=True)
            gout[base + i] = jnp.broadcast_to(gate, gout.shape[1:])

        @pl.loop(0, pieces)
        def _(j):
            cols = pl.ds(pl.multiple_of(j * COLS, COLS), COLS)
            grads = lax.dot_general(
                gpu[zz], wgu[cols, :], (((1,), (1,)), ((), ())), preferred_element_type=jnp.float32
            )
            part[pl.ds(base, column), :, cols] = grads.astype(jnp.bfloat16).reshape(column, cap, COLS)

    def add_half(zz, yy, to):
        source = index_of(zz, yy, c)
        h_copy(zz, yy).wait_recv()

        @pl.loop(0, pieces)
        def _(j):
            cols = pl.ds(pl.multiple_of(j * COLS, COLS), COLS)
            pairs[zz, to, :, cols] = (
                part[source, :, cols].astype(jnp.float32) + half[zz, yy, :, cols].astype(jnp.float32)
            ).astype(jnp.bfloat16)

    def gate_row(i, fn):
        pl.when(i != me)(lambda: fn(i))

    def spread(zz, j):
        cols = pl.ds(pl.multiple_of(j * COLS, COLS), COLS)
        hot = onehot_rows(metas, index_of(zz, y, c), own, other, cap)
        rows = jnp.concatenate([pairs[zz, 0, :, cols], pairs[zz, 1, :, cols]], axis=0)
        total = lax.dot_general(hot, rows, (((0,), (0,)), ((), ())), preferred_element_type=jnp.float32)
        return total.astype(jnp.bfloat16)

    def add_came(value, zz, way, j):
        arrived(came.at[zz, way, j], r_recv.at[zz, way, j])
        return (value.astype(jnp.float32) + came[zz, way, j].astype(jnp.float32)).astype(jnp.bfloat16)

    def chain(zz, relayed):
        way = jnp.where(zz < z, 0, 1)
        p_copy(zz).wait_recv()

        @pl.loop(0, pieces)
        def _(j):
            value = spread(zz, j)
            dense[zz, j] = add_came(value, zz, way, j) if relayed else value
            r_copy(zz, way, j).start()

    middle = (z > 0) & (z < NZ - 1)

    def process(zz):
        for a in range(2):
            relay(zz, a)
        for a in range(2):
            for yy in range(NY):
                c_copy(index_of(zz, yy, 1 - c), a).wait_recv()
        block(zz)
        for i in range(NY):
            h_copy(zz, (1 - y + i) % NY).start()
        for i in range(column):
            gate_row(zz * column + i, lambda target: q_copy(target).start())
        add_half(zz, 1 - y, 2)
        p_copy(zz).start()
        add_half(zz, y, 0)

    long_side = 1 - 2 * (z // 2)

    def send_own_g(side):
        pl.when((side == 1) & (z < NZ - 1))(lambda: up_copy(z, 1).start())
        pl.when((side == -1) & (z > 0))(lambda: dn_copy(z, 1).start())

    loads[0].wait()
    forward(z, 0)
    loads[1].wait()
    pl.when(jnp.logical_not(middle))(lambda: send_own_g(long_side))

    def give_meta(i, carry):
        meta_copy(me, (me + i) % NS).start()
        return carry

    def take_meta(i, carry):
        source = (me + i) % NS
        meta_copy(source, source).wait_recv()
        return carry

    lax.fori_loop(1, NS, give_meta, 0)
    lax.fori_loop(1, NS, take_meta, 0)

    @pl.loop(0, NZ)
    def _(d):
        def step(zz):
            @pl.when(d > 0)
            def _():
                arrived(zbuf.at[zz, 0], z_recv.at[zz, 0])
                forward(zz, 0)

            pick(zz, 0)

        both_ways(d, step)

    pick(z, 1)
    for load in loads[2:]:
        load.wait()

    @pl.loop(0, NZ)
    def _(k):
        come = z + long_side * jnp.where(middle, jnp.where(k == 0, -1, NZ - 1 - k), NZ - k)

        @pl.when((middle & (k < NZ - 1)) | (jnp.logical_not(middle) & (k > 0)))
        def _():
            arrived(zbuf.at[come, 1], z_recv.at[come, 1])
            forward(come, 1)
            pl.when(middle & (k == 0))(lambda: send_own_g(long_side))
            pl.when(middle & (k == NZ - 2))(lambda: send_own_g(-long_side))
            pick(come, 1)

        pl.when(jnp.logical_not(middle) & (k > 1))(lambda: chain(z + long_side * (NZ + 1 - k), False))
        process(z + long_side * jnp.where(k == 0, 0, jnp.where(middle & (k == 1), -1, NZ - k)))

    pl.when(jnp.logical_not(middle))(lambda: chain(z + long_side, False))

    @pl.when(middle)
    def _():
        chain(z + 2 * long_side, True)
        chain(z - long_side, True)

    @pl.loop(0, width // TILE)
    def _(j):
        cols = pl.ds(pl.multiple_of(j * TILE, TILE), TILE)
        wide = jnp.zeros((TILE, 2 * hidden), jnp.float32)
        down = jnp.zeros((hidden, TILE), jnp.float32)
        for k in range(NZ):
            rows_x = slots[0, k * column : (k + 1) * column, :, cols].reshape(rows_col, TILE)
            wide += lax.dot_general(
                rows_x, gpu[k], (((0,), (0,)), ((), ())), preferred_element_type=jnp.float32
            )
            rows_g = slots[1, k * column : (k + 1) * column, :, cols].reshape(rows_col, TILE)
            scaled = (prob[k] * rows_g.astype(jnp.float32)).astype(jnp.bfloat16)
            down += jnp.dot(hid_t[k], scaled, preferred_element_type=jnp.float32)
        gate_out[cols, :] = wide[:, :hidden].astype(jnp.bfloat16)
        up_out[cols, :] = wide[:, hidden:].astype(jnp.bfloat16)
        down_out[:, cols] = down.astype(jnp.bfloat16)

    @pl.when(middle)
    def _():
        chain(z + long_side, True)

    p_copy(z).wait_recv()

    @pl.loop(0, pieces)
    def _(j):
        cols = pl.ds(pl.multiple_of(j * COLS, COLS), COLS)
        token_ref[:, cols] = spread(z, j)

        @pl.when(z < NZ - 1)
        def _():
            token_ref[:, cols] = add_came(token_ref[:, cols], z, 0, j)

        @pl.when(z > 0)
        def _():
            token_ref[:, cols] = add_came(token_ref[:, cols], z, 1, j)

    gates[me] = gout[me]

    def finish(zz, carry):
        for a in range(2):

            @pl.when((zz <= z) & (z < NZ - 1))
            def _():
                up_copy(zz, a).wait_send()

            @pl.when((zz >= z) & (z > 0))
            def _():
                dn_copy(zz, a).wait_send()

            y_copy(zz, a).wait_send()
            for yy in range(NY):
                c_copy(index_of(zz, yy, c), a).wait_send()
        for yy in range(NY):
            h_copy(zz, yy).wait_send()
        p_copy(zz).wait_send()

        @pl.when(zz != z)
        def _():
            for j in range(pieces):
                r_copy(zz, jnp.where(zz < z, 0, 1), j).wait_send()

        return carry

    lax.fori_loop(0, NZ, finish, 0)

    def done(i, carry):
        target = (me + i) % NS
        meta_copy(me, target).wait_send()
        q_copy(target).wait_send()
        arrived(gates.at[target], q_recv.at[target])
        return carry

    lax.fori_loop(1, NS, done, 0)


def route_tables(route_probs, expert_ids, experts):
    tok_count = expert_ids.shape[0]
    names = jnp.arange(experts, dtype=jnp.int32)
    hit = expert_ids.T[:, None, :] == names[None, :, None]
    routed = jnp.any(hit, axis=0)
    order = jnp.arange(tok_count, dtype=jnp.int32)
    before = (order[:, None] < order[None, :]).astype(jnp.bfloat16)
    rank = jnp.dot(routed.astype(jnp.bfloat16), before, preferred_element_type=jnp.float32)
    slot = jnp.where(routed, rank, -1.0)
    prob = jnp.sum(jnp.where(hit, route_probs.T.astype(jnp.float32)[:, None, :], 0.0), axis=0)
    return hit, jnp.concatenate([slot, prob], axis=0)


def local_chips(tokens, cotangent, route_probs, expert_ids, w_gate, w_up, w_down):
    tok_count, d_model = tokens.shape
    per_token = expert_ids.shape[1]
    experts = NS // 2
    cap = 2 * (tok_count * per_token // experts)
    hit, meta = route_tables(route_probs, expert_ids, experts)
    hidden = w_down.shape[1]
    column = NY * NC
    pieces = d_model // COLS
    vmem = pl.BlockSpec(memory_space=pltpu.VMEM)
    hbm = pl.BlockSpec(memory_space=pl.ANY)
    dma = pltpu.SemaphoreType.DMA
    half_type = jnp.bfloat16
    token_grad, gates, gate_grad, up_grad, down_grad = pl.pallas_call(
        fused_kernel,
        out_shape=(
            jax.ShapeDtypeStruct((tok_count, d_model), half_type),
            jax.ShapeDtypeStruct((NS, 8, tok_count), jnp.float32),
            jax.ShapeDtypeStruct((d_model, hidden), half_type),
            jax.ShapeDtypeStruct((d_model, hidden), half_type),
            jax.ShapeDtypeStruct((hidden, d_model), half_type),
        ),
        in_specs=[hbm, hbm, vmem, hbm, hbm, hbm],
        out_specs=(vmem,) * 5,
        scratch_shapes=[
            pltpu.VMEM((NS,) + meta.shape, jnp.float32),
            pltpu.VMEM((NZ, 2, tok_count, d_model), half_type),
            pltpu.VMEM((2, NZ, cap, d_model), half_type),
            pltpu.VMEM((2, NS, cap, d_model), half_type),
            pltpu.VMEM((d_model, 2 * hidden), half_type),
            pltpu.VMEM((hidden, d_model), half_type),
            pltpu.VMEM((NZ, column * cap, 2 * hidden), half_type),
            pltpu.VMEM((NZ, hidden, column * cap), half_type),
            pltpu.VMEM((NZ, column * cap, 1), jnp.float32),
            pltpu.VMEM((NS, cap, d_model), half_type),
            pltpu.VMEM((NS, 8, tok_count), jnp.float32),
            pltpu.VMEM((NZ, NY, cap, d_model), half_type),
            pltpu.VMEM((NZ, 3, cap, d_model), half_type),
            pltpu.VMEM((NZ, pieces, tok_count, COLS), half_type),
            pltpu.VMEM((NZ, 2, pieces, tok_count, COLS), half_type),
            dma((5,)),
            dma((NS,)),
            dma((NS,)),
            dma((NZ, 2)),
            dma((NZ, 2)),
            dma((NZ, 2)),
            dma((2, NZ)),
            dma((2, NZ)),
            dma((2, NS)),
            dma((2, NS)),
            dma((NZ, NY)),
            dma((NZ, NY)),
            dma((NS,)),
            dma((NS,)),
            dma((NZ,)),
            dma((NZ,)),
            dma((NZ, pieces)),
            dma((NZ, 2, pieces)),
        ],
        compiler_params=pltpu.CompilerParams(
            collective_id=0, has_side_effects=True, vmem_limit_bytes=LIMIT
        ),
    )(tokens, cotangent, meta, w_gate[0], w_up[0], w_down[0])
    both = gates[:, 0, :].reshape(experts, 2, tok_count).sum(axis=1)
    prob_grad = jnp.sum(jnp.where(hit, both[None], 0.0), axis=1).T.astype(jnp.bfloat16)
    return (token_grad, prob_grad, gate_grad[None], up_grad[None], down_grad[None])


def solution(mesh):
    in_specs = (
        P(("groups", "expert"), None),
        P(("groups", "expert"), None),
        P(("groups", "expert"), None),
        P(("groups", "expert"), None),
        P(("groups", "expert"), None, None),
        P(("groups", "expert"), None, None),
        P(("groups", "expert"), None, None),
    )
    out_specs = (
        P(("groups", "expert"), None),
        P(("groups", "expert"), None),
        P(("groups", "expert"), None, None),
        P(("groups", "expert"), None, None),
        P(("groups", "expert"), None, None),
    )
    body = local_chips if mesh.shape["expert"] == NS else local
    return jax.shard_map(body, mesh=mesh, in_specs=in_specs, out_specs=out_specs, check_vma=False)
```

```python
import jax
import jax.numpy as jnp
from jax import lax
from jax.experimental import pallas as pl
from jax.experimental.pallas import tpu as pltpu
from jax.sharding import PartitionSpec as P


def half_backward(rows_x, rows_g, rows_p, gate_half, up_half, down_half):
    pre_gate = jnp.dot(rows_x, gate_half, preferred_element_type=jnp.float32)
    pre_up = jnp.dot(rows_x, up_half, preferred_element_type=jnp.float32)
    sigma = jax.nn.sigmoid(pre_gate)
    active = pre_gate * sigma
    hidden = (active * pre_up).astype(jnp.bfloat16)
    back_hidden = jnp.dot(rows_g, down_half.T, preferred_element_type=jnp.float32)
    gate_part = jnp.sum(back_hidden * hidden.astype(jnp.float32), axis=1).astype(jnp.bfloat16)
    weight_rows = rows_p.astype(jnp.float32)[:, None]
    scaled_hidden = weight_rows * back_hidden
    grad_pre = (scaled_hidden * pre_up * sigma * (1.0 + pre_gate * (1.0 - sigma))).astype(
        jnp.bfloat16
    )
    grad_up = (scaled_hidden * active).astype(jnp.bfloat16)
    scaled_cot = (weight_rows * rows_g.astype(jnp.float32)).astype(jnp.bfloat16)
    down_grad = jnp.dot(hidden.T, scaled_cot, preferred_element_type=jnp.float32).astype(
        jnp.bfloat16
    )
    gate_grad = jnp.dot(rows_x.T, grad_pre, preferred_element_type=jnp.float32).astype(jnp.bfloat16)
    up_grad = jnp.dot(rows_x.T, grad_up, preferred_element_type=jnp.float32).astype(jnp.bfloat16)
    input_part = (
        jnp.dot(grad_pre, gate_half.T, preferred_element_type=jnp.float32)
        + jnp.dot(grad_up, up_half.T, preferred_element_type=jnp.float32)
    ).astype(jnp.bfloat16)
    return (input_part, gate_part, gate_grad, up_grad, down_grad)


def local(tokens, cotangent, route_probs, expert_ids, w_gate, w_up, w_down):
    tok_count = tokens.shape[0]
    d_model = tokens.shape[1]
    per_token = expert_ids.shape[1]
    devices = lax.axis_size("expert")
    experts = devices // 2
    capacity = 2 * (tok_count * per_token // experts)
    pair_count = tok_count * per_token
    flat_ids = expert_ids.reshape(-1)
    onehot = (flat_ids[:, None] == jnp.arange(experts, dtype=jnp.int32)[None, :]).astype(jnp.int32)
    ranks = jnp.sum((jnp.cumsum(onehot, axis=0) - 1) * onehot, axis=1)
    place = flat_ids * capacity + ranks
    source = (
        jnp.full((experts * capacity,), pair_count, jnp.int32)
        .at[place]
        .set(jnp.arange(pair_count, dtype=jnp.int32))
    )
    tok_pad = jnp.concatenate([tokens, jnp.zeros((1, d_model), tokens.dtype)], axis=0)
    cot_pad = jnp.concatenate([cotangent, jnp.zeros((1, d_model), cotangent.dtype)], axis=0)
    prob_pad = jnp.concatenate(
        [route_probs.reshape(-1), jnp.zeros((1,), route_probs.dtype)], axis=0
    )
    send_x = tok_pad[source // per_token]
    send_g = cot_pad[source // per_token]
    send_p = prob_pad[source]
    got_x, got_g, got_p = (
        lax.all_to_all(
            jnp.repeat(send_x.reshape(experts, capacity, d_model), 2, axis=0),
            "expert",
            split_axis=0,
            concat_axis=0,
            tiled=True,
        ),
        lax.all_to_all(
            jnp.repeat(send_g.reshape(experts, capacity, d_model), 2, axis=0),
            "expert",
            split_axis=0,
            concat_axis=0,
            tiled=True,
        ),
        lax.all_to_all(
            jnp.repeat(send_p.reshape(experts, capacity), 2, axis=0),
            "expert",
            split_axis=0,
            concat_axis=0,
            tiled=True,
        ),
    )
    input_part, gate_part, gate_grad, up_grad, down_grad = half_backward(
        got_x.reshape(-1, d_model),
        got_g.reshape(-1, d_model),
        got_p.reshape(-1),
        w_gate[0],
        w_up[0],
        w_down[0],
    )
    part_rows = input_part.reshape(devices, capacity, d_model)
    part_gate = gate_part.reshape(devices, capacity)
    back_rows, back_gate = (
        lax.all_to_all(part_rows, "expert", split_axis=0, concat_axis=0, tiled=True),
        lax.all_to_all(part_gate, "expert", split_axis=0, concat_axis=0, tiled=True),
    )
    result_rows = (
        back_rows.reshape(experts, 2, capacity, d_model)
        .astype(jnp.float32)
        .sum(axis=1)
        .astype(jnp.bfloat16)
        .reshape(-1, d_model)
    )
    result_gate = (
        back_gate.reshape(experts, 2, capacity)
        .astype(jnp.float32)
        .sum(axis=1)
        .astype(jnp.bfloat16)
        .reshape(-1)
    )
    pair_rows = result_rows[place]
    token_grad = (
        pair_rows.reshape(tok_count, per_token, d_model)
        .astype(jnp.float32)
        .sum(axis=1)
        .astype(jnp.bfloat16)
    )
    prob_grad = result_gate[place].reshape(tok_count, per_token)
    return (token_grad, prob_grad, gate_grad[None], up_grad[None], down_grad[None])


NZ, NY, NC = 4, 2, 2
NS = NZ * NY * NC
COLS = 1024
WIDE = 2048
TILE = 256
LIMIT = 56 * 2**20


def place_of(index):
    return index // (NY * NC), (index // NC) % NY, index % NC


def index_of(z, y, c):
    return z * (NY * NC) + y * NC + c


def enter(me):
    barrier = pltpu.get_barrier_semaphore()

    def greet(i, carry):
        pl.semaphore_signal(
            barrier, inc=1, device_id={"expert": (me + i) % NS}, device_id_type=pl.DeviceIdType.MESH
        )
        return carry

    lax.fori_loop(1, NS, greet, 0)
    pl.semaphore_wait(barrier, NS - 1)


def remote(src, dst, send, recv, target):
    return pltpu.make_async_remote_copy(
        src_ref=src,
        dst_ref=dst,
        send_sem=send,
        recv_sem=recv,
        device_id={"expert": target},
        device_id_type=pl.DeviceIdType.MESH,
    )


def onehot_rows(metas, source, own, other, cap):
    slot = lax.broadcasted_iota(jnp.int32, (cap, metas.shape[2]), 0).astype(jnp.float32)
    mine = metas[source, pl.ds(own, 1), :]
    theirs = metas[source, pl.ds(other, 1), :]
    return jnp.concatenate([slot == mine, slot == theirs], axis=0).astype(jnp.bfloat16)


def fused_kernel(
    x_ref, g_ref, meta_ref, wg_ref, wu_ref, wd_ref,
    token_ref, gates, gate_out, up_out, down_out,
    metas, zbuf, ysend, slots, wgu, wd, gpu, hid_t, prob, part, gout, half, pairs, dense, came,
    loc_sem, meta_send, meta_recv, up_send, dn_send, z_recv, y_send, y_recv, c_send, c_recv,
    h_send, h_recv, q_send, q_recv, p_send, p_recv, r_send, r_recv,
):
    me = lax.axis_index("expert")
    z, y, c = place_of(me)
    own, other = z * NY + y, z * NY + (1 - y)
    experts = NS // 2
    cap, width = slots.shape[2], slots.shape[3]
    hidden = wd.shape[0]
    column = NY * NC
    rows_col = column * cap
    pieces = width // COLS
    loads = (
        pltpu.make_async_copy(x_ref, zbuf.at[z, 0], loc_sem.at[0]),
        pltpu.make_async_copy(g_ref, zbuf.at[z, 1], loc_sem.at[1]),
        pltpu.make_async_copy(wg_ref, wgu.at[:, pl.ds(0, hidden)], loc_sem.at[2]),
        pltpu.make_async_copy(wu_ref, wgu.at[:, pl.ds(hidden, hidden)], loc_sem.at[3]),
        pltpu.make_async_copy(wd_ref, wd, loc_sem.at[4]),
    )
    for load in loads:
        load.start()
    metas[me] = meta_ref[...]
    enter(me)

    def meta_copy(source, target):
        return remote(metas.at[source], metas.at[source], meta_send.at[target], meta_recv.at[source], target)

    def up_copy(zz, a):
        return remote(
            zbuf.at[zz, a], zbuf.at[zz, a], up_send.at[zz, a], z_recv.at[zz, a], index_of(z + 1, y, c)
        )

    def dn_copy(zz, a):
        return remote(
            zbuf.at[zz, a], zbuf.at[zz, a], dn_send.at[zz, a], z_recv.at[zz, a], index_of(z - 1, y, c)
        )

    def y_copy(zz, a):
        return remote(
            ysend.at[a, zz],
            slots.at[a, index_of(zz, y, c)],
            y_send.at[a, zz],
            y_recv.at[a, zz],
            index_of(z, 1 - y, c),
        )

    def c_copy(source, a):
        return remote(
            slots.at[a, source],
            slots.at[a, source],
            c_send.at[a, source],
            c_recv.at[a, source],
            index_of(z, y, 1 - c),
        )

    def h_copy(zz, yy):
        return remote(
            part.at[index_of(zz, yy, 1 - c)],
            half.at[zz, yy],
            h_send.at[zz, yy],
            h_recv.at[zz, yy],
            index_of(z, y, 1 - c),
        )

    def q_copy(target):
        return remote(gout.at[target], gates.at[me], q_send.at[target], q_recv.at[me], target)

    def p_copy(zz):
        return remote(
            pairs.at[zz, 2], pairs.at[zz, 1], p_send.at[zz], p_recv.at[zz], index_of(z, 1 - y, c)
        )

    def r_copy(zz, way, j):
        return remote(
            dense.at[zz, j],
            came.at[zz, way, j],
            r_send.at[zz, j],
            r_recv.at[zz, way, j],
            index_of(z - 1 + 2 * way, y, c),
        )

    def arrived(ref, sem):
        pltpu.make_async_copy(ref, ref, sem).wait()

    def both_ways(d, fn):
        @pl.loop(0, 2)
        def _(way):
            zz = z - d + 2 * d * way
            pl.when((zz >= 0) & (zz < NZ) & ((d > 0) | (way == 0)))(lambda: fn(zz))

    def forward(zz, a):
        @pl.when((zz <= z) & (z < NZ - 1))
        def _():
            up_copy(zz, a).start()

        @pl.when((zz >= z) & (z > 0))
        def _():
            dn_copy(zz, a).start()

    def pick(zz, a):
        source = index_of(zz, y, c)
        hot = onehot_rows(metas, source, own, other, cap)

        @pl.loop(0, width // WIDE)
        def _(j):
            cols = pl.ds(pl.multiple_of(j * WIDE, WIDE), WIDE)
            rows = jnp.dot(hot, zbuf[zz, a, :, cols], preferred_element_type=jnp.float32)
            rows = rows.astype(jnp.bfloat16)
            slots[a, source, :, cols] = rows[:cap]
            ysend[a, zz, :, cols] = rows[cap:]

        y_copy(zz, a).start()
        c_copy(source, a).start()

    def relay(zz, a):
        source = index_of(zz, 1 - y, c)
        arrived(slots.at[a, source], y_recv.at[a, zz])
        c_copy(source, a).start()

    def block(zz):
        base = zz * column
        hots = []
        probs = []
        for i in range(column):
            row = metas[base + i, pl.ds(own, 1), :]
            slot = lax.broadcasted_iota(jnp.int32, (cap, row.shape[1]), 0).astype(jnp.float32)
            hots.append(slot == row)
            weight = metas[base + i, pl.ds(own + experts, 1), :]
            probs.append(jnp.sum(jnp.where(hots[i], weight, 0.0), axis=1, keepdims=True))
        p = jnp.concatenate(probs, axis=0)
        prob[zz] = p
        rows_x = slots[0, pl.ds(base, column)].reshape(rows_col, width)
        pre = jnp.dot(rows_x, wgu[...], preferred_element_type=jnp.float32)
        pre_gate, pre_up = pre[:, :hidden], pre[:, hidden:]
        rows_g = slots[1, pl.ds(base, column)].reshape(rows_col, width)
        back = lax.dot_general(
            rows_g, wd[...], (((1,), (1,)), ((), ())), preferred_element_type=jnp.float32
        )
        sigma = jax.nn.sigmoid(pre_gate)
        active = pre_gate * sigma
        hid = (active * pre_up).astype(jnp.bfloat16)
        q = jnp.sum(back * hid.astype(jnp.float32), axis=1, keepdims=True)
        q = q.astype(jnp.bfloat16).astype(jnp.float32)
        scaled = p * back
        gpu[zz, :, :hidden] = (
            scaled * pre_up * sigma * (1.0 + pre_gate * (1.0 - sigma))
        ).astype(jnp.bfloat16)
        gpu[zz, :, hidden:] = (scaled * active).astype(jnp.bfloat16)
        hid_t[zz] = hid.T
        for i in range(column):
            gate = jnp.sum(jnp.where(hots[i], q[i * cap : (i + 1) * cap], 0.0), axis=0, keepdims=True)
            gout[base + i] = jnp.broadcast_to(gate, gout.shape[1:])

        @pl.loop(0, pieces)
        def _(j):
            cols = pl.ds(pl.multiple_of(j * COLS, COLS), COLS)
            grads = lax.dot_general(
                gpu[zz], wgu[cols, :], (((1,), (1,)), ((), ())), preferred_element_type=jnp.float32
            )
            part[pl.ds(base, column), :, cols] = grads.astype(jnp.bfloat16).reshape(column, cap, COLS)

    def add_half(zz, yy, to):
        source = index_of(zz, yy, c)
        h_copy(zz, yy).wait_recv()

        @pl.loop(0, width // WIDE)
        def _(j):
            cols = pl.ds(pl.multiple_of(j * WIDE, WIDE), WIDE)
            pairs[zz, to, :, cols] = (
                part[source, :, cols].astype(jnp.float32) + half[zz, yy, :, cols].astype(jnp.float32)
            ).astype(jnp.bfloat16)

    def gate_row(i, fn):
        pl.when(i != me)(lambda: fn(i))

    def spread(zz, j):
        cols = pl.ds(pl.multiple_of(j * COLS, COLS), COLS)
        hot = onehot_rows(metas, index_of(zz, y, c), own, other, cap)
        rows = jnp.concatenate([pairs[zz, 0, :, cols], pairs[zz, 1, :, cols]], axis=0)
        total = lax.dot_general(hot, rows, (((0,), (0,)), ((), ())), preferred_element_type=jnp.float32)
        return total.astype(jnp.bfloat16)

    def add_came(value, zz, way, j):
        arrived(came.at[zz, way, j], r_recv.at[zz, way, j])
        return (value.astype(jnp.float32) + came[zz, way, j].astype(jnp.float32)).astype(jnp.bfloat16)

    def chain(zz, relayed):
        way = jnp.where(zz < z, 0, 1)
        p_copy(zz).wait_recv()

        @pl.loop(0, pieces)
        def _(j):
            value = spread(zz, j)
            dense[zz, j] = add_came(value, zz, way, j) if relayed else value
            r_copy(zz, way, j).start()

    middle = (z > 0) & (z < NZ - 1)

    def process(zz):
        for a in range(2):
            relay(zz, a)
        for a in range(2):
            for yy in range(NY):
                c_copy(index_of(zz, yy, 1 - c), a).wait_recv()
        block(zz)
        for i in range(NY):
            h_copy(zz, (1 - y + i) % NY).start()
        for i in range(column):
            gate_row(zz * column + i, lambda target: q_copy(target).start())
        add_half(zz, 1 - y, 2)
        p_copy(zz).start()
        add_half(zz, y, 0)

    long_side = 1 - 2 * (z // 2)

    def send_own_g(side):
        pl.when((side == 1) & (z < NZ - 1))(lambda: up_copy(z, 1).start())
        pl.when((side == -1) & (z > 0))(lambda: dn_copy(z, 1).start())

    loads[0].wait()
    forward(z, 0)
    loads[1].wait()
    pl.when(jnp.logical_not(middle))(lambda: send_own_g(long_side))

    def give_meta(i, carry):
        meta_copy(me, (me + i) % NS).start()
        return carry

    def take_meta(i, carry):
        source = (me + i) % NS
        meta_copy(source, source).wait_recv()
        return carry

    lax.fori_loop(1, NS, give_meta, 0)
    lax.fori_loop(1, NS, take_meta, 0)

    @pl.loop(0, NZ)
    def _(d):
        def step(zz):
            @pl.when(d > 0)
            def _():
                arrived(zbuf.at[zz, 0], z_recv.at[zz, 0])
                forward(zz, 0)

            pick(zz, 0)

        both_ways(d, step)

    pick(z, 1)
    for load in loads[2:]:
        load.wait()

    @pl.loop(0, NZ)
    def _(k):
        come = z + long_side * jnp.where(middle, jnp.where(k == 0, -1, NZ - 1 - k), NZ - k)

        @pl.when((middle & (k < NZ - 1)) | (jnp.logical_not(middle) & (k > 0)))
        def _():
            arrived(zbuf.at[come, 1], z_recv.at[come, 1])
            forward(come, 1)
            pl.when(middle & (k == 0))(lambda: send_own_g(long_side))
            pl.when(middle & (k == NZ - 2))(lambda: send_own_g(-long_side))
            pick(come, 1)

        pl.when(jnp.logical_not(middle) & (k > 1))(lambda: chain(z + long_side * (NZ + 1 - k), False))
        process(z + long_side * jnp.where(k == 0, 0, jnp.where(middle & (k == 1), -1, NZ - k)))

    pl.when(jnp.logical_not(middle))(lambda: chain(z + long_side, False))

    @pl.when(middle)
    def _():
        chain(z + 2 * long_side, True)
        chain(z - long_side, True)

    @pl.loop(0, width // TILE)
    def _(j):
        cols = pl.ds(pl.multiple_of(j * TILE, TILE), TILE)
        wide = jnp.zeros((TILE, 2 * hidden), jnp.float32)
        down = jnp.zeros((hidden, TILE), jnp.float32)
        for k in range(NZ):
            rows_x = slots[0, k * column : (k + 1) * column, :, cols].reshape(rows_col, TILE)
            wide += lax.dot_general(
                rows_x, gpu[k], (((0,), (0,)), ((), ())), preferred_element_type=jnp.float32
            )
            rows_g = slots[1, k * column : (k + 1) * column, :, cols].reshape(rows_col, TILE)
            scaled = (prob[k] * rows_g.astype(jnp.float32)).astype(jnp.bfloat16)
            down += jnp.dot(hid_t[k], scaled, preferred_element_type=jnp.float32)
        gate_out[cols, :] = wide[:, :hidden].astype(jnp.bfloat16)
        up_out[cols, :] = wide[:, hidden:].astype(jnp.bfloat16)
        down_out[:, cols] = down.astype(jnp.bfloat16)

    @pl.when(middle)
    def _():
        chain(z + long_side, True)

    p_copy(z).wait_recv()

    @pl.loop(0, pieces)
    def _(j):
        cols = pl.ds(pl.multiple_of(j * COLS, COLS), COLS)
        token_ref[:, cols] = spread(z, j)

        @pl.when(z < NZ - 1)
        def _():
            token_ref[:, cols] = add_came(token_ref[:, cols], z, 0, j)

        @pl.when(z > 0)
        def _():
            token_ref[:, cols] = add_came(token_ref[:, cols], z, 1, j)

    gates[me] = gout[me]

    def finish(zz, carry):
        for a in range(2):

            @pl.when((zz <= z) & (z < NZ - 1))
            def _():
                up_copy(zz, a).wait_send()

            @pl.when((zz >= z) & (z > 0))
            def _():
                dn_copy(zz, a).wait_send()

            y_copy(zz, a).wait_send()
            for yy in range(NY):
                c_copy(index_of(zz, yy, c), a).wait_send()
        for yy in range(NY):
            h_copy(zz, yy).wait_send()
        p_copy(zz).wait_send()

        @pl.when(zz != z)
        def _():
            for j in range(pieces):
                r_copy(zz, jnp.where(zz < z, 0, 1), j).wait_send()

        return carry

    lax.fori_loop(0, NZ, finish, 0)

    def done(i, carry):
        target = (me + i) % NS
        meta_copy(me, target).wait_send()
        q_copy(target).wait_send()
        arrived(gates.at[target], q_recv.at[target])
        return carry

    lax.fori_loop(1, NS, done, 0)


def route_tables(route_probs, expert_ids, experts):
    tok_count = expert_ids.shape[0]
    names = jnp.arange(experts, dtype=jnp.int32)
    hit = expert_ids.T[:, None, :] == names[None, :, None]
    routed = jnp.any(hit, axis=0)
    order = jnp.arange(tok_count, dtype=jnp.int32)
    before = (order[:, None] < order[None, :]).astype(jnp.bfloat16)
    rank = jnp.dot(routed.astype(jnp.bfloat16), before, preferred_element_type=jnp.float32)
    slot = jnp.where(routed, rank, -1.0)
    prob = jnp.sum(jnp.where(hit, route_probs.T.astype(jnp.float32)[:, None, :], 0.0), axis=0)
    return hit, jnp.concatenate([slot, prob], axis=0)


def local_chips(tokens, cotangent, route_probs, expert_ids, w_gate, w_up, w_down):
    tok_count, d_model = tokens.shape
    per_token = expert_ids.shape[1]
    experts = NS // 2
    cap = 2 * (tok_count * per_token // experts)
    hit, meta = route_tables(route_probs, expert_ids, experts)
    hidden = w_down.shape[1]
    column = NY * NC
    pieces = d_model // COLS
    vmem = pl.BlockSpec(memory_space=pltpu.VMEM)
    hbm = pl.BlockSpec(memory_space=pl.ANY)
    dma = pltpu.SemaphoreType.DMA
    half_type = jnp.bfloat16
    token_grad, gates, gate_grad, up_grad, down_grad = pl.pallas_call(
        fused_kernel,
        out_shape=(
            jax.ShapeDtypeStruct((tok_count, d_model), half_type),
            jax.ShapeDtypeStruct((NS, 8, tok_count), jnp.float32),
            jax.ShapeDtypeStruct((d_model, hidden), half_type),
            jax.ShapeDtypeStruct((d_model, hidden), half_type),
            jax.ShapeDtypeStruct((hidden, d_model), half_type),
        ),
        in_specs=[hbm, hbm, vmem, hbm, hbm, hbm],
        out_specs=(vmem,) * 5,
        scratch_shapes=[
            pltpu.VMEM((NS,) + meta.shape, jnp.float32),
            pltpu.VMEM((NZ, 2, tok_count, d_model), half_type),
            pltpu.VMEM((2, NZ, cap, d_model), half_type),
            pltpu.VMEM((2, NS, cap, d_model), half_type),
            pltpu.VMEM((d_model, 2 * hidden), half_type),
            pltpu.VMEM((hidden, d_model), half_type),
            pltpu.VMEM((NZ, column * cap, 2 * hidden), half_type),
            pltpu.VMEM((NZ, hidden, column * cap), half_type),
            pltpu.VMEM((NZ, column * cap, 1), jnp.float32),
            pltpu.VMEM((NS, cap, d_model), half_type),
            pltpu.VMEM((NS, 8, tok_count), jnp.float32),
            pltpu.VMEM((NZ, NY, cap, d_model), half_type),
            pltpu.VMEM((NZ, 3, cap, d_model), half_type),
            pltpu.VMEM((NZ, pieces, tok_count, COLS), half_type),
            pltpu.VMEM((NZ, 2, pieces, tok_count, COLS), half_type),
            dma((5,)),
            dma((NS,)),
            dma((NS,)),
            dma((NZ, 2)),
            dma((NZ, 2)),
            dma((NZ, 2)),
            dma((2, NZ)),
            dma((2, NZ)),
            dma((2, NS)),
            dma((2, NS)),
            dma((NZ, NY)),
            dma((NZ, NY)),
            dma((NS,)),
            dma((NS,)),
            dma((NZ,)),
            dma((NZ,)),
            dma((NZ, pieces)),
            dma((NZ, 2, pieces)),
        ],
        compiler_params=pltpu.CompilerParams(
            collective_id=0, has_side_effects=True, vmem_limit_bytes=LIMIT
        ),
    )(tokens, cotangent, meta, w_gate[0], w_up[0], w_down[0])
    both = gates[:, 0, :].reshape(experts, 2, tok_count).sum(axis=1)
    prob_grad = jnp.sum(jnp.where(hit, both[None], 0.0), axis=1).T.astype(jnp.bfloat16)
    return (token_grad, prob_grad, gate_grad[None], up_grad[None], down_grad[None])


def solution(mesh):
    in_specs = (
        P(("groups", "expert"), None),
        P(("groups", "expert"), None),
        P(("groups", "expert"), None),
        P(("groups", "expert"), None),
        P(("groups", "expert"), None, None),
        P(("groups", "expert"), None, None),
        P(("groups", "expert"), None, None),
    )
    out_specs = (
        P(("groups", "expert"), None),
        P(("groups", "expert"), None),
        P(("groups", "expert"), None, None),
        P(("groups", "expert"), None, None),
        P(("groups", "expert"), None, None),
    )
    body = local_chips if mesh.shape["expert"] == NS else local
    return jax.shard_map(body, mesh=mesh, in_specs=in_specs, out_specs=out_specs, check_vma=False)
```
